32 devices in a mesh: batch: 4 (over y, x), seq: 4 (over z), chip: 2 (over core).
Axes of the slice: x: 2, y: 2, z: 4, core: 2. Of those that a mesh axis runs over, the one named last changes fastest.
Arguments:
- tokens: bfloat16 [4096, 2048], P(('batch', 'seq', 'chip')), may hold values from -6 to 6
- starts: int32 [4096], P(('batch', 'seq', 'chip')), may hold values from 0 to 1, as said below
- w_query: bfloat16 [2048, 2048], P(('batch', 'seq', 'chip')), may hold values from -0.125 to 0.125
- w_forget: bfloat16 [2048, 2048], P(('batch', 'seq', 'chip')), may hold values from -0.125 to 0.125
- w_input: bfloat16 [2048, 2048], P(('batch', 'seq', 'chip')), may hold values from -0.125 to 0.125
- w_output: bfloat16 [2048, 2048], P(('batch', 'seq', 'chip')), may hold values from -0.125 to 0.125
- gain_mix: float32 [2048], P(('batch', 'seq', 'chip')), may hold values from 0.5 to 1.5
- lower_bound: float32 [2048], P(('batch', 'seq', 'chip')), may hold values from 0.9 to 0.9995
- gain_state: float32 [2048], P(('batch', 'seq', 'chip')), may hold values from 0.5 to 1.5
- w_gate: bfloat16 [2048, 5632], P(('batch', 'seq', 'chip')), may hold values from -0.125 to 0.125
- w_up: bfloat16 [2048, 5632], P(('batch', 'seq', 'chip')), may hold values from -0.125 to 0.125
- w_down: bfloat16 [5632, 2048], P(('batch', 'seq', 'chip')), may hold values from -0.078125 to 0.078125
- gain_ffn: float32 [2048], P(('batch', 'seq', 'chip')), may hold values from 0.5 to 1.5
- cotangent: bfloat16 [4096, 2048], P(('batch', 'seq', 'chip')), may hold values from -6 to 6
Outputs:
- output: bfloat16 [4096, 2048], P(('batch', 'seq', 'chip'))
- grad_tokens: float32 [4096, 2048], P(('batch', 'seq', 'chip'))
- grad_query: float32 [2048, 2048], P(('batch', 'seq', 'chip'))
- grad_forget: float32 [2048, 2048], P(('batch', 'seq', 'chip'))
- grad_input: float32 [2048, 2048], P(('batch', 'seq', 'chip'))
- grad_output: float32 [2048, 2048], P(('batch', 'seq', 'chip'))
- grad_gain_mix: float32 [2048], P(('batch', 'seq', 'chip'))
- grad_lower: float32 [2048], P(('batch', 'seq', 'chip'))
- grad_gain_state: float32 [2048], P(('batch', 'seq', 'chip'))
- grad_gate: float32 [2048, 5632], P(('batch', 'seq', 'chip'))
- grad_up: float32 [2048, 5632], P(('batch', 'seq', 'chip'))
- grad_down: float32 [5632, 2048], P(('batch', 'seq', 'chip'))
- grad_gain_ffn: float32 [2048], P(('batch', 'seq', 'chip'))
The draws below stay inside these ranges and needn't reach their ends.
Inputs may be any that keep to these rules, and one draw needn't show every extreme that they name: `starts`: in each group's 1024 rows (counted from 0) a document begins at row 0 and at exactly two more rows: one at a row from 1 to 127, one at a row from 896 to 1023.
All inputs are finite; a program needn't handle non-finite values.
Results may differ from the reference program's by a relative error of at most 0.0095.
Values may be sent and summed in bfloat16 or wider, within the bound.
No kernel may reach another device: no remote copies, remote signals or barrier semaphores. Data moves between devices by JAX's collectives and lax.ppermute only.
A program may use at most 448 MiB of HBM per device.

```python
import jax
import jax.numpy as jnp
from jax import lax

D = 2048
FF = 5632
HDIM = 128
HEADS = 16
BLOCK = 64
TOK_DEV = 128
SEQ_LEN = 1024
GROUPS = 4
TOKENS = 4096


def draw_starts(key, part):
    first_break = jax.random.randint(jax.random.fold_in(key, 11), (GROUPS, 1), 1, TOK_DEV)
    last_break = jax.random.randint(jax.random.fold_in(key, 12), (GROUPS, 1), SEQ_LEN - TOK_DEV, SEQ_LEN)
    position = jnp.arange(SEQ_LEN)[None, :]
    boundary = (position == 0) | (position == first_break) | (position == last_break)
    return boundary.astype(jnp.int32).reshape(GROUPS * SEQ_LEN)


def level_of(key, dims, cuts, smallest, high):
    factor_of = 1.0
    for dim, shards_of in cuts:
        heights = jax.random.uniform(jax.random.fold_in(jax.random.fold_in(key, 6), dim), (shards_of,), jnp.float32, smallest / len(cuts), high / len(cuts))
        factor_of = factor_of * jnp.repeat(jnp.exp(heights), dims[dim] // shards_of).reshape((-1,) + (1,) * (len(dims) - 1 - dim))
    return factor_of


def normal_values(key, shape, deviation, most, cuts=(), held_as=jnp.bfloat16):
    entries = jax.random.normal(key, shape, jnp.float32) * deviation
    if len(cuts) > 0:
        entries = level_of(key, shape, cuts, -0.22, 0.18) * entries
    return jnp.clip(entries, min=-most, max=most).astype(held_as)


def setup_inputs(seed: int = 0) -> dict:
    arg_keys = jax.random.split(jax.random.key(seed), 15)
    tokens = normal_values(arg_keys[0], (TOKENS, D), 1.0, 6.0, ((0, 32),))
    starts = draw_starts(jax.random.fold_in(arg_keys[14], 71), 0)
    w_query = normal_values(arg_keys[2], (D, D), D ** -0.5, 0.125, ((0, 32),))
    w_forget = normal_values(arg_keys[3], (D, D), D ** -0.5, 0.125, ((0, 32),))
    w_input = normal_values(arg_keys[4], (D, D), D ** -0.5, 0.125, ((0, 32),))
    w_output = normal_values(arg_keys[5], (D, D), D ** -0.5, 0.125, ((0, 32),))
    gain_mix = jnp.clip(1.0 + 0.1 * jax.random.normal(arg_keys[6], (D,), jnp.float32), 0.5, 1.5)
    lower_bound = jnp.clip(0.9 + 0.0995 * jax.random.uniform(arg_keys[7], (D,), jnp.float32) ** level_of(arg_keys[7], (D,), ((0, 32),), -0.2, 0.2), 0.9, 0.9995)
    gain_state = jnp.clip(1.0 + 0.1 * jax.random.normal(arg_keys[8], (D,), jnp.float32), 0.5, 1.5)
    w_gate = normal_values(arg_keys[9], (D, FF), D ** -0.5, 0.125, ((0, 32),))
    w_up = normal_values(arg_keys[10], (D, FF), D ** -0.5, 0.125, ((0, 32),))
    w_down = normal_values(arg_keys[11], (FF, D), FF ** -0.5, 0.078125, ((0, 32),))
    gain_ffn = jnp.clip(1.0 + 0.1 * jax.random.normal(arg_keys[12], (D,), jnp.float32), 0.5, 1.5)
    cotangent = normal_values(arg_keys[13], (TOKENS, D), 1.0, 6.0, ((0, 32),))
    return {"tokens": tokens, "starts": starts, "w_query": w_query, "w_forget": w_forget, "w_input": w_input, "w_output": w_output, "gain_mix": gain_mix, "lower_bound": lower_bound, "gain_state": gain_state, "w_gate": w_gate, "w_up": w_up, "w_down": w_down, "gain_ffn": gain_ffn, "cotangent": cotangent}


EPSILON = 1e-06
RESET_LOG = -30.0
EXACT_PRECISION = lax.Precision.HIGHEST

@jax.custom_vjp
def low(v):
    return lax.optimization_barrier(v.astype(jnp.bfloat16)).astype(jnp.float32)

@jax.custom_vjp
def low_back(v):
    return v

def low_keep(v):
    return (low(v), None)

def low_pass(kept, grad):
    return (grad,)

def back_keep(v):
    return (v, None)

def back_low(kept, grad):
    return (low(grad),)
low.defvjp(low_keep, low_pass)
low_back.defvjp(back_keep, back_low)

def root_norm(values, gain):
    return values * lax.rsqrt(lax.optimization_barrier(jnp.mean(values * values, axis=-1, keepdims=True)) + EPSILON) * gain

def precise_dot(left, right):
    return jnp.dot(left, right, precision=EXACT_PRECISION, preferred_element_type=jnp.float32)

def block_step(incoming_state, pieces):
    query_act, key_act, value_activation, log_decay = pieces
    cumulative = jnp.cumsum(log_decay, axis=0)
    query_expansion = query_act * jnp.exp(cumulative)
    key_shrink = key_act * jnp.exp(-cumulative)
    scores = jnp.einsum('thk,shk->hts', query_expansion, key_shrink, precision=EXACT_PRECISION)
    block_rows = query_act.shape[0]
    causal = jnp.arange(block_rows)[:, None] >= jnp.arange(block_rows)[None, :]
    scores = jnp.where(causal[None], scores, 0.0)
    output_values = jnp.einsum('hts,shv->thv', scores, value_activation, precision=EXACT_PRECISION)
    output_values = output_values + jnp.einsum('aju,jup->ajp', query_expansion, incoming_state, precision=EXACT_PRECISION)
    block_count_total = cumulative[-1]
    key_suffix_factor = key_act * jnp.exp(block_count_total[None] - cumulative)
    outgoing_state = jnp.exp(block_count_total)[..., None] * incoming_state + jnp.einsum('lcg,lcw->cgw', key_suffix_factor, value_activation, precision=EXACT_PRECISION)
    return (outgoing_state, output_values)

def recurrence(query_act, key_act, value_activation, log_decay):

    def blocks(array):
        return jnp.moveaxis(array.reshape(GROUPS, SEQ_LEN // BLOCK, BLOCK, HEADS, HDIM), 1, 0)
    stepper = jax.checkpoint(jax.vmap(block_step))
    zero_state = jnp.zeros((GROUPS, HEADS, HDIM, HDIM), jnp.float32)
    final_state, block_outs = lax.scan(stepper, zero_state, (blocks(query_act), blocks(key_act), blocks(value_activation), blocks(log_decay)))
    return jnp.moveaxis(block_outs, 0, 1).reshape(GROUPS * SEQ_LEN, HEADS * HDIM)

def layer(tokens, w_query, w_forget, w_input, w_output, gain_mix, lower_bound, gain_state, w_gate, w_up, w_down, gain_ffn, starts):
    normed_in = low(root_norm(tokens, gain_mix))
    query_pre = low_back(precise_dot(normed_in, w_query))
    forget_pre = low_back(precise_dot(normed_in, w_forget))
    value_activation = low_back(precise_dot(normed_in, w_input))
    query_act = jax.nn.silu(query_pre)
    forget_gate = lower_bound + (1.0 - lower_bound) * jax.nn.sigmoid(forget_pre)
    key_act = 1.0 - forget_gate
    log_decay = jnp.where(starts[:, None] == 1, RESET_LOG, jnp.log(forget_gate))
    mixed = recurrence(query_act, key_act, value_activation, log_decay)
    normed_mix = low(root_norm(mixed, gain_state))
    residual = tokens + low_back(precise_dot(normed_mix, w_output))
    normed_ffn = low(root_norm(residual, gain_ffn))
    gate_act = low_back(precise_dot(normed_ffn, w_gate))
    up_act = low_back(precise_dot(normed_ffn, w_up))
    hidden = low(jax.nn.silu(gate_act) * up_act)
    return residual + low_back(precise_dot(hidden, w_down))

def reference(tokens, starts, w_query, w_forget, w_input, w_output, gain_mix, lower_bound, gain_state, w_gate, w_up, w_down, gain_ffn, cotangent):
    floats = tuple((array.astype(jnp.float32) for array in (tokens, w_query, w_forget, w_input, w_output, gain_mix, lower_bound, gain_state, w_gate, w_up, w_down, gain_ffn)))

    def forward(*arrays):
        return layer(*arrays, starts)
    output, pullback = jax.vjp(forward, *floats)
    grads = pullback(cotangent.astype(jnp.float32))
    return (output.astype(jnp.bfloat16), grads[0], grads[1], grads[2], grads[3], grads[4], grads[5], grads[6], grads[7], grads[8], grads[9], grads[10], grads[11])
```

```python
import jax
import jax.numpy as jnp
from jax import lax
from jax.sharding import PartitionSpec as P

HDIM = 128
EPSILON = 1e-06
RESET_LOG = -30.0
EXACT = lax.Precision.HIGHEST
F32 = jnp.float32
LOW = jnp.bfloat16
AXES = ("batch", "seq", "chip")


def dot(left, right):
    return jnp.dot(left, right, preferred_element_type=F32)


def dot_tn(left, right):
    return lax.dot_general(left, right, (((0,), (0,)), ((), ())), preferred_element_type=F32)


def dot_nt(left, right):
    return lax.dot_general(left, right, (((1,), (1,)), ((), ())), preferred_element_type=F32)


def inverse_rms(values):
    return lax.rsqrt(jnp.mean(values * values, axis=-1, keepdims=True) + EPSILON)


def norm_back(values, rms, scaled):
    inner = jnp.mean(scaled * values, axis=-1, keepdims=True)
    return rms * scaled - values * (rms * rms * rms * inner)


def pick(flag, first, second):
    return jnp.where(flag, first, second)


def body(
    tokens, starts, w_query, w_forget, w_input, w_output, gain_mix, lower_bound, gain_state,
    w_gate, w_up, w_down, gain_ffn, cotangent,
):
    nb, ns, nc = (lax.axis_size(a) for a in AXES)
    b, s, c = (lax.axis_index(a) for a in AXES)
    rows, width = tokens.shape
    r = w_query.shape[0]
    part = width // (nb * nc)
    ffr = w_down.shape[0]
    heads = part // HDIM
    span = nc * rows

    def from_batch(x, k):
        return lax.ppermute(x, "batch", [(i, i ^ k) for i in range(nb)])

    def from_core(x):
        return lax.ppermute(x, "chip", [(i, i ^ 1) for i in range(nc)])

    def turn(x):
        return lax.ppermute(x, "seq", [(i, (i + 1) % ns) for i in range(ns)])

    def unmixed(blocks):
        out = [list(row) for row in blocks]
        bit = 1
        while bit < nb:
            on = (b & bit) != 0
            out = [[pick(on, out[i ^ bit][j], out[i][j]) for j in range(nc)] for i in range(nb)]
            bit *= 2
        on = c != 0
        return [[pick(on, out[i][j ^ 1], out[i][j]) for j in range(nc)] for i in range(nb)]

    def gather_plane(x):
        mine = jnp.stack([x] + [from_batch(x, k) for k in range(1, nb)])
        return jnp.stack([mine, from_core(mine)], axis=1)

    def scatter_plane(x):
        both = x[:, 0] + from_core(x[:, 1].astype(LOW)).astype(F32)
        total = both[0]
        sent = both[1:].astype(LOW)
        for k in range(1, nb):
            total = total + from_batch(sent[k - 1], k).astype(F32)
        return total

    def spread_columns(x):
        own = lax.dynamic_index_in_dim(x, c, 2, keepdims=False)
        other = from_core(lax.dynamic_index_in_dim(x, c ^ 1, 2, keepdims=False))
        got = []
        for k in range(nb):
            pair = jnp.stack([lax.dynamic_index_in_dim(y, b ^ k, 1, keepdims=False) for y in (own, other)])
            pair = from_batch(pair, k) if k else pair
            got.append([pair[0], pair[1]])
        return jnp.stack([jnp.stack(row) for row in unmixed(got)])

    def collect_columns(x):
        x = x.astype(LOW)
        got = []
        for k in range(nb):
            y = lax.dynamic_index_in_dim(x, b ^ k, 0, keepdims=False)
            got.append(from_batch(y, k) if k else y)
        got = jnp.stack(got)
        own = lax.dynamic_index_in_dim(got, c, 1, keepdims=False)
        other = from_core(lax.dynamic_index_in_dim(got, c ^ 1, 1, keepdims=False))
        return unmixed([[own[k], other[k]] for k in range(nb)])

    def ring_gather(x, axis):
        shape = x.shape[:axis] + (ns,) + x.shape[axis:]
        out = jnp.zeros(shape, x.dtype)
        for k in range(ns):
            if k:
                x = turn(x)
            out = lax.dynamic_update_index_in_dim(out, x, (s - k) % ns, axis)
        return out

    def ring_scatter(x, axis):
        def block(k):
            return lax.dynamic_index_in_dim(x, (s - k) % ns, axis, keepdims=False)

        total = block(1 % ns)
        for k in range(2, ns + 1):
            total = turn(total.astype(LOW)).astype(F32) + block(k % ns)
        return total

    by_part = lambda w: w.reshape(r, nb, nc, part)
    by_unit = lambda w: w.reshape(r, nb, ns, nc, ffr).transpose(0, 1, 3, 2, 4).reshape(r, nb, nc, ns * ffr)
    forget_value = spread_columns(jnp.concatenate([by_part(w_forget), by_part(w_input)], axis=3))
    small = jnp.concatenate(
        [gain_mix, gain_state, gain_ffn, lower_bound, starts.astype(F32)]
    ).reshape(1, -1)
    plane_small = gather_plane(small)[:, :, 0]
    plane_starts = plane_small[:, :, 4 * r :].reshape(nb, span)
    vectors = [[plane_small[i, j, : 4 * r].reshape(4, r) for j in range(nc)] for i in range(nb)]
    vectors = jnp.stack([jnp.stack(row, axis=1) for row in unmixed(vectors)], axis=1)
    vectors = ring_gather(vectors, 2).reshape(4, width)
    full_gain_mix, full_gain_state, full_gain_ffn, full_lower = (vectors[i] for i in range(4))
    lower_part = lax.dynamic_slice_in_dim(full_lower, (b * nc + c) * part, part)

    plane_tokens = gather_plane(tokens).reshape(nb * span, width)
    forget_value = ring_gather(forget_value, 1).reshape(width, 2 * part)
    query_low = spread_columns(by_part(w_query))
    query_low = ring_gather(query_low, 1).reshape(width, part)
    gate_up = spread_columns(jnp.concatenate([by_unit(w_gate), by_unit(w_up)], axis=3))
    full_output = lax.all_gather(w_output, AXES, axis=0, tiled=True)
    units = ns * ffr
    gate_up = ring_gather(gate_up, 1).reshape(width, 2 * units)
    down = ring_gather(w_down, 0).reshape(units, width)
    plane_cotangent = gather_plane(cotangent).reshape(nb * span, width)

    values = plane_tokens.astype(F32)
    normed_in = (values * inverse_rms(values) * full_gain_mix).astype(LOW)
    forget_value_pre = dot(normed_in, forget_value)
    query_pre = dot(normed_in, query_low)
    split = lambda x: x.reshape(nb, span, heads, HDIM)
    lower = lower_part.reshape(heads, HDIM)
    forget_sig = jax.nn.sigmoid(split(forget_value_pre[:, :part]))
    value_act = split(forget_value_pre[:, part:])
    query_pre = split(query_pre)
    query_sig = jax.nn.sigmoid(query_pre)
    query_act = query_pre * query_sig
    forget_gate = lower + (1.0 - lower) * forget_sig
    key_act = 1.0 - forget_gate
    is_start = plane_starts[:, :, None, None] == 1.0
    log_decay = jnp.where(is_start, 0.0, jnp.log(forget_gate))

    place = jnp.arange(span)
    place = ((place // rows) ^ c) * rows + place % rows
    causal = (place[:, None] >= place[None, :]).astype(F32)
    cumulative = jnp.einsum("ts,gshk->gthk", causal, log_decay, precision=EXACT)
    count = jnp.einsum("ts,gs->gt", causal, plane_starts, precision=EXACT)
    total = jnp.sum(log_decay, axis=1)
    total_count = jnp.sum(plane_starts, axis=1)
    reach = jnp.exp(RESET_LOG * count)[:, :, None, None]
    left = jnp.exp(RESET_LOG * (total_count[:, None] - count))[:, :, None, None]
    mask = causal[None] * jnp.exp(RESET_LOG * jnp.maximum(count[:, :, None] - count[:, None, :], 0.0))
    mask = mask[:, None]
    grow = jnp.exp(cumulative)
    shrink = jnp.exp(-cumulative)
    suffix = jnp.exp(total[:, None] - cumulative) * left
    decay = jnp.exp(total + RESET_LOG * total_count[:, None, None])[..., None]
    query_ext = (query_act * grow).astype(LOW)
    key_shrink = (key_act * shrink).astype(LOW)
    key_suffix = (key_act * suffix).astype(LOW)
    value_low = value_act.astype(LOW)
    es = lambda spec, x, y: jnp.einsum(spec, x, y, preferred_element_type=F32)
    end_state = es("gthk,gthv->ghkv", key_suffix, value_low)

    def carry(local, step):
        incoming = jnp.zeros_like(local)
        for _ in range(ns - 1):
            pairs = [(i, i + step) for i in range(ns) if 0 <= i + step < ns]
            incoming = lax.ppermute((decay * incoming + local).astype(LOW), "seq", pairs).astype(F32)
        return incoming

    incoming = carry(end_state, 1)
    incoming_low = incoming.astype(LOW)
    scores = (es("gthk,gshk->ghts", query_ext, key_shrink) * mask).astype(LOW)
    mixed = es("ghts,gshv->gthv", scores, value_low)
    mixed = mixed + reach * es("gthk,ghkv->gthv", query_ext, incoming_low)

    def to_tokens(x):
        x = x.reshape(nb, nc, rows, part)
        got = jnp.stack([x[0]] + [from_batch(x[k], k) for k in range(1, nb)])
        other = from_core(got[:, 1])
        blocks = unmixed([[got[k, 0], other[k]] for k in range(nb)])
        return jnp.concatenate([y for row in blocks for y in row], axis=1)

    def to_parts(x):
        blocks = unmixed(
            [[x[:, (i * nc + j) * part : (i * nc + j + 1) * part] for j in range(nc)] for i in range(nb)]
        )
        own = jnp.stack([row[0] for row in blocks])
        other = from_core(jnp.stack([row[1] for row in blocks]))
        both = jnp.stack([own, other], axis=1)
        return jnp.stack([both[0]] + [from_batch(both[k], k) for k in range(1, nb)])

    mixed_own = to_tokens(mixed.astype(LOW)).astype(F32)
    own_tokens = tokens.astype(F32)
    mix_rms = inverse_rms(mixed_own)
    normed_mix = (mixed_own * mix_rms * full_gain_state).astype(LOW)
    residual = own_tokens + dot(normed_mix, full_output)
    ffn_rms = inverse_rms(residual)
    normed_ffn = (residual * ffn_rms * full_gain_ffn).astype(LOW)

    plane_ffn = gather_plane(normed_ffn).reshape(nb * span, width)
    gate_up_act = dot(plane_ffn, gate_up)
    gate_act, up_act = gate_up_act[:, :units], gate_up_act[:, units:]
    gate_sig = jax.nn.sigmoid(gate_act)
    gate_silu = gate_act * gate_sig
    hidden = (gate_silu * up_act).astype(LOW)
    grad_hidden = dot_nt(plane_cotangent, down)
    grad_gate_act = (grad_hidden * up_act * gate_sig * (1.0 + gate_act * (1.0 - gate_sig))).astype(LOW)
    grad_up_act = (grad_hidden * gate_silu).astype(LOW)
    grad_gate_up = jnp.concatenate([grad_gate_act, grad_up_act], axis=1)
    by_plane = lambda x: x.reshape(nb, nc, rows, width)
    grad_normed_ffn = scatter_plane(by_plane(dot_nt(grad_gate_up, gate_up)))
    output = (residual + scatter_plane(by_plane(dot(hidden, down)))).astype(LOW)

    grad_residual = cotangent.astype(F32) + norm_back(residual, ffn_rms, grad_normed_ffn * full_gain_ffn)
    grad_branch = grad_residual.astype(LOW)
    grad_mixed = norm_back(mixed_own, mix_rms, dot_nt(grad_branch, full_output) * full_gain_state)
    grad_mixed = to_parts(grad_mixed.astype(LOW)).reshape(nb, span, heads, HDIM)

    grad_down = ring_scatter(dot_tn(hidden, plane_cotangent).reshape(ns, ffr, width), 0)
    grad_gate_up = ring_scatter(dot_tn(plane_ffn, grad_gate_up).reshape(nb, ns, nc * r, 2 * units), 1)

    grad_reach = (reach * grad_mixed.astype(F32)).astype(LOW)
    grad_next = carry(es("gthk,gthv->ghkv", query_ext, grad_reach), -1)
    next_low = grad_next.astype(LOW)
    grad_scores = (es("gthv,gshv->ghts", grad_mixed, value_low) * mask).astype(LOW)
    grad_ext = es("ghts,gshk->gthk", grad_scores, key_shrink) + es("gthv,ghkv->gthk", grad_reach, incoming_low)
    grad_shrink = es("ghts,gthk->gshk", grad_scores, query_ext)
    grad_suffix = es("gthv,ghkv->gthk", value_low, next_low)
    grad_value = es("ghts,gthv->gshv", scores, grad_mixed) + es("gthk,ghkv->gthv", key_suffix, next_low)
    grad_query = grad_ext * grow
    grad_key = grad_shrink * shrink + grad_suffix * suffix
    suffix_term = key_suffix.astype(F32) * grad_suffix
    grad_cumulative = query_ext.astype(F32) * grad_ext - key_shrink.astype(F32) * grad_shrink - suffix_term
    grad_total = jnp.sum(suffix_term, axis=1) + jnp.sum(decay * incoming * grad_next, axis=-1)
    grad_log = jnp.einsum("ts,gthk->gshk", causal, grad_cumulative, precision=EXACT) + grad_total[:, None]
    grad_forget = jnp.where(is_start, 0.0, grad_log / forget_gate) - grad_key
    grad_lower = jnp.sum(grad_forget * (1.0 - forget_sig), axis=(0, 1)).reshape(1, part)
    grad_query_pre = grad_query * query_sig * (1.0 + query_pre * (1.0 - query_sig))
    grad_forget_pre = grad_forget * (1.0 - lower) * forget_sig * (1.0 - forget_sig)
    flat = lambda x: x.reshape(nb * span, part).astype(LOW)
    grad_pre = jnp.concatenate([flat(grad_forget_pre), flat(grad_value), flat(grad_query_pre)], axis=1)
    projections = jnp.concatenate([forget_value, query_low], axis=1)
    grad_normed_in = scatter_plane(by_plane(dot_nt(grad_pre, projections)))
    grad_tokens = grad_residual + norm_back(own_tokens, inverse_rms(own_tokens), grad_normed_in * full_gain_mix)
    grad_projections = ring_scatter(dot_tn(normed_in, grad_pre).reshape(nb, ns, nc * r, 3 * part), 1)

    plane_mix = to_parts(normed_mix).reshape(nb * span, part)
    plane_branch = gather_plane(grad_branch).reshape(nb * span, width)
    grad_out = dot_tn(plane_mix, plane_branch).reshape(ns // nc, nc, r, width)
    own = lax.dynamic_index_in_dim(grad_out, c, 1, keepdims=False)
    other = from_core(lax.dynamic_index_in_dim(grad_out, c ^ 1, 1, keepdims=False).astype(LOW)).astype(F32)
    grad_out = pick(c == 0, jnp.concatenate([own, other]), jnp.concatenate([other, own]))
    grad_output = ring_scatter(grad_out, 0)

    blocks = collect_columns(grad_projections.reshape(nb, nc, r, 3 * part))
    columns = lambda i: jnp.concatenate(
        [y[:, i * part : (i + 1) * part] for row in blocks for y in row], axis=1
    ).astype(F32)
    grad_w_forget, grad_w_input, grad_w_query = columns(0), columns(1), columns(2)
    blocks = collect_columns(grad_gate_up.reshape(nb, nc, r, 2 * units))
    blocks = jnp.stack([jnp.stack(row) for row in blocks]).reshape(nb, nc, r, 2, ns, ffr)
    grad_w_gate, grad_w_up = (
        blocks[:, :, :, i].transpose(2, 0, 3, 1, 4).reshape(r, w_gate.shape[1]).astype(F32) for i in range(2)
    )
    shifts = [grad_lower] + [
        lax.ppermute(grad_lower, "seq", [(i, (i + k) % ns) for i in range(ns)]) for k in range(1, ns)
    ]
    grad_lower = sum(shifts)
    other = from_core(grad_lower)
    grad_lower = pick(c == 0, jnp.concatenate([grad_lower, other], 1), jnp.concatenate([other, grad_lower], 1))[0]
    grad_lower = lax.dynamic_slice_in_dim(grad_lower, (s * nc + c) * r, r)

    def along(*pairs):
        return sum(jnp.sum(w.astype(F32) * g, axis=1) for w, g in pairs)

    grad_gain_mix = along((w_query, grad_w_query), (w_forget, grad_w_forget), (w_input, grad_w_input)) / gain_mix
    grad_gain_state = along((w_output, grad_output)) / gain_state
    grad_gain_ffn = along((w_gate, grad_w_gate), (w_up, grad_w_up)) / gain_ffn
    return (
        output, grad_tokens, grad_w_query, grad_w_forget, grad_w_input, grad_output, grad_gain_mix, grad_lower,
        grad_gain_state, grad_w_gate, grad_w_up, grad_down, grad_gain_ffn,
    )


def solution(mesh):
    flat, matrix = P(AXES), P(AXES, None)
    return jax.shard_map(
        body,
        mesh=mesh,
        in_specs=(
            matrix, flat, matrix, matrix, matrix, matrix, flat, flat, flat, matrix, matrix, matrix, flat, matrix,
        ),
        out_specs=(
            matrix, matrix, matrix, matrix, matrix, matrix, flat, flat, flat, matrix, matrix, matrix, flat,
        ),
        check_vma=False,
    )
```

```python
import math
from functools import partial

import jax
import jax.numpy as jnp
from jax import lax
from jax.experimental import pallas as pl
from jax.experimental.pallas import tpu as pltpu
from jax.sharding import PartitionSpec as P

HDIM = 128
EPSILON = 1e-06
RESET_LOG = -30.0
F32 = jnp.float32
LOW = jnp.bfloat16
AXES = ("y", "x", "h", "l", "chip")
LIMIT = 56 * 2**20
VMEM = pl.BlockSpec(memory_space=pltpu.VMEM)
SMEM = pl.BlockSpec(memory_space=pltpu.SMEM)
ANY = pl.BlockSpec(memory_space=pl.ANY)


def dot(left, right):
    return jnp.dot(left, right, preferred_element_type=F32)


def dot_tn(left, right):
    return lax.dot_general(left, right, (((0,), (0,)), ((), ())), preferred_element_type=F32)


def dot_nt(left, right):
    return lax.dot_general(left, right, (((1,), (1,)), ((), ())), preferred_element_type=F32)


def inverse_rms(values):
    return lax.rsqrt(jnp.mean(values * values, axis=-1, keepdims=True) + EPSILON)


def norm_back(values, rms, scaled):
    inner = jnp.mean(scaled * values, axis=-1, keepdims=True)
    return rms * scaled - values * (rms * rms * rms * inner)


def sigmoid(a):
    return 1.0 / (1.0 + jnp.exp(-a))


def pick(flag, first, second):
    return jnp.where(flag, first, second)


def after(x, *deps):
    return lax.optimization_barrier((x, deps))[0]


def shape(dims, dtype=F32):
    return jax.ShapeDtypeStruct(tuple(dims), dtype)


def call(kernel, outs, *args, specs=None, out_specs=None, grid=(), scratch=(), flops=0):
    outs = tuple(outs)
    specs = [VMEM] * len(args) if specs is None else specs
    out_specs = tuple([VMEM] * len(outs)) if out_specs is None else tuple(out_specs)
    moved = sum(math.prod(a.shape) * a.dtype.itemsize for a in (*args, *outs))
    return pl.pallas_call(
        kernel,
        out_shape=outs,
        grid=grid,
        in_specs=specs,
        out_specs=out_specs,
        scratch_shapes=list(scratch),
        compiler_params=pltpu.CompilerParams(vmem_limit_bytes=LIMIT),
        cost_estimate=pl.CostEstimate(flops=int(flops), bytes_accessed=int(moved), transcendentals=0),
    )(*args)


class Plan:
    def __init__(self, sizes):
        self.ny, self.nx, self.nh, self.nl, self.nc = sizes
        self.plane = self.nx * self.nl
        self.copies = self.ny * self.nh
        self.devices = self.copies * self.plane * self.nc

    def owner(self, y, p, h, c):
        return (((y * self.nx + p // self.nl) * self.nh + h) * self.nl + p % self.nl) * self.nc + c


def fetch(plan, where, blocks, target, sems, start=True):
    y, h, here = (where[i] for i in range(3))
    moves = []
    for t, (source, i, j, k, e) in enumerate(blocks):
        yy = lax.rem(y + (plan.ny - j), plan.ny)
        hh = lax.rem(h + (plan.nh - i), plan.nh)
        place = plan.owner(yy, here ^ k, hh, e)
        move = pltpu.make_async_copy(source, target.at[place], sems.at[t])
        if start:
            move.start()
        moves.append(move)
    return moves


def pack_kernel(plan, ffr, gate, up, out):
    units = plan.copies * ffr
    for e in range(plan.nc):
        for p in range(plan.plane):
            for w, base in ((gate, 0), (up, units)):
                for m in range(plan.copies):
                    at = plan.owner(m // plan.nh, p, m % plan.nh, e) * ffr
                    to = base + m * ffr
                    out[e, p, :, to : to + ffr] = w[:, at : at + ffr]


def unpack_kernel(plan, ffr, where, blocks, gate, up, grad_gate, grad_up, along, ordered):
    here = where[2]
    units = plan.copies * ffr
    for k in range(plan.plane):
        for e in range(plan.nc):
            ordered[e, here ^ k] = blocks[e, k]
    for e in range(plan.nc):
        for p in range(plan.plane):
            block = ordered[e, p].astype(F32)
            for g, base in ((grad_gate, 0), (grad_up, units)):
                for m in range(plan.copies):
                    at = plan.owner(m // plan.nh, p, m % plan.nh, e) * ffr
                    to = base + m * ffr
                    g[:, at : at + ffr] = block[:, to : to + ffr]
    total = jnp.sum(gate[...].astype(F32) * grad_gate[...], axis=1, keepdims=True)
    total = total + jnp.sum(up[...].astype(F32) * grad_up[...], axis=1, keepdims=True)
    along[...] = jnp.broadcast_to(total, along.shape)


def unpack_part_kernel(plan, part, where, blocks, w0, w1, w2, g0, g1, g2, along):
    here = where[2]
    for k in range(plan.plane):
        for e in range(plan.nc):
            at = pl.multiple_of(((here ^ k) * plan.nc + e) * part, part)
            for i, g in enumerate((g0, g1, g2)):
                g[:, pl.ds(at, part)] = blocks[e, k, :, i * part : (i + 1) * part].astype(F32)
    total = 0.0
    for w, g in ((w0, g0), (w1, g1), (w2, g2)):
        total = total + jnp.sum(w[...].astype(F32) * g[...], axis=1, keepdims=True)
    along[...] = jnp.broadcast_to(total, along.shape)


def normalize(x, gain, out, step):
    @pl.loop(0, x.shape[0] // step)
    def _(t):
        at = pl.ds(pl.multiple_of(t * step, step), step)
        values = x[at, :].astype(F32)
        out[at, :] = (values * inverse_rms(values) * gain[...]).astype(LOW)


def project_kernel(plan, names, where, x, gain, *rest):
    blocks, (normed, pre, weight, sems) = rest[: len(names)], rest[len(names) :]
    moves = fetch(
        plan, where,
        [(ref.at[k * plan.nc + e], i, j, k, e) for ref, (i, j) in zip(blocks, names)
         for k in range(plan.plane) for e in range(plan.nc)],
        weight, sems,
    )
    normalize(x, gain, normed, 64)
    for move in moves:
        move.wait()
    pre[...] = dot(normed[...], weight[...].reshape(-1, weight.shape[-1]))


def ffn_kernel(plan, names, where, normed, cotangent, down, *rest):
    blocks, (hidden, grad_gu, part_out, part_grad, weight, sems) = rest[: len(names)], rest[len(names) :]
    first = pl.program_id(0) == 0

    def moves(start):
        return fetch(
            plan, where,
            [(ref.at[i, k * plan.nc + e], i, j, base + k, e) for ref, (j, base) in zip(blocks, names)
             for i in range(plan.nh) for k in range(ref.shape[1] // plan.nc) for e in range(plan.nc)],
            weight, sems, start,
        )

    @pl.when(first)
    def _():
        moves(True)

    units = down.shape[0]
    upstream = dot_nt(cotangent[...], down[...])

    @pl.when(first)
    def _():
        for move in moves(False):
            move.wait()

    full = weight[...].reshape(-1, weight.shape[-1])
    both = dot(normed[...], full)
    gate, up = both[:, :units], both[:, units:]
    sig = sigmoid(gate)
    silu = gate * sig
    hid = (silu * up).astype(LOW)
    hidden[...] = hid
    grad_gu[:, :units] = (upstream * up * sig * (1.0 + gate * (1.0 - sig))).astype(LOW)
    grad_gu[:, units:] = (upstream * silu).astype(LOW)
    part_grad[...] = dot_nt(grad_gu[...], full).astype(part_grad.dtype)
    part_out[...] = dot(hid, down[...]).astype(part_out.dtype)


def columns_grad_kernel(plan, turn, sides, count, where, normed, *rest):
    grads, out = rest[:count], rest[count]
    y = lax.rem(where[0] + (plan.ny - turn), plan.ny)
    step = out.shape[0] * out.shape[2]
    for t, side in enumerate(sides):
        at = pl.multiple_of((y * plan.nx + (where[5] ^ side)) * step, step)
        base = 0
        for a in grads:
            n = a.shape[1]
            value = dot_tn(normed[:, pl.ds(at, step)], a[...])
            for i in range(plan.nh):
                out[i, t, :, base : base + n] = value[i * out.shape[2] : (i + 1) * out.shape[2]].astype(out.dtype)
            base += n


def rows_grad_kernel(left, right, out):
    n = 512
    for t in range(out.shape[1] // n):
        at = slice(t * n, (t + 1) * n)
        out[:, at] = dot_tn(left[...], right[:, at]).astype(out.dtype)


def interleaved(x):
    return jnp.concatenate([x[e, 0, i] for i in range(x.shape[2]) for e in range(x.shape[0])], axis=0)


def separated(x, out):
    nc, _, nl, rows, _ = out.shape
    for i in range(nl):
        for e in range(nc):
            at = (i * nc + e) * rows
            out[e, 0, i] = x[at : at + rows].astype(out.dtype)


def thirds(x):
    first = x.astype(LOW)
    rest = x - first.astype(F32)
    second = rest.astype(LOW)
    return first, second, (rest - second.astype(F32)).astype(LOW)


def causal_of(where, span, rows):
    flip = where[4] * rows
    t = lax.broadcasted_iota(jnp.int32, (span, span), 0) ^ flip
    s = lax.broadcasted_iota(jnp.int32, (span, span), 1) ^ flip
    return (t >= s).astype(F32)


def gate_terms(forget_pre, lower, is_start):
    sig = sigmoid(forget_pre)
    gate = lower + (1.0 - lower) * sig
    return sig, gate, 1.0 - gate, jnp.where(is_start, 0.0, jnp.log(gate))


def decay_terms(causal, starts, starts_row, cumulative, total):
    low = causal.astype(LOW)
    count = dot(low, starts)
    count_row = dot_nt(starts_row, low)[:1]
    ends = jnp.sum(starts.astype(F32), axis=0, keepdims=True)
    reach = jnp.exp(RESET_LOG * count)
    left = jnp.exp(RESET_LOG * (ends - count))
    between = causal * jnp.exp(RESET_LOG * jnp.maximum(count[:, :1] - count_row, 0.0))
    return reach, between, jnp.exp(cumulative), jnp.exp(-cumulative), jnp.exp(total - cumulative) * left, ends


def mix_kernel(
    where, f, v, q, lower, starts, starts_row,
    end_state, decay, local, query_reach, cumulative_out, scores_out,
):
    rows = f.shape[3]
    forget_pre, value, query_pre = interleaved(f), interleaved(v), interleaved(q)
    span = forget_pre.shape[0]
    is_start = starts[0].astype(F32) == 1.0
    _, _, key, log_decay = gate_terms(forget_pre, lower[0], is_start)
    causal = causal_of(where, span, rows)
    low = causal.astype(LOW)
    parts = thirds(log_decay)
    cumulative = dot(low, parts[0]) + dot(low, parts[1]) + dot(low, parts[2])
    total = jnp.sum(log_decay, axis=0, keepdims=True)
    reach, between, grow, shrink, suffix, ends = decay_terms(causal, starts[0], starts_row[0], cumulative, total)
    query = query_pre * sigmoid(query_pre) * grow
    value_low = value.astype(LOW)
    end_state[0, 0] = dot_tn((key * suffix).astype(LOW), value_low)
    ones = jnp.ones((span, HDIM), LOW)
    total_column = dot_tn(parts[0], ones) + dot_tn(parts[1], ones) + dot_tn(parts[2], ones)
    decay[0, 0] = jnp.exp(total_column + RESET_LOG * ends)
    scores = (dot_nt(query.astype(LOW), (key * shrink).astype(LOW)) * between).astype(LOW)
    local[0, 0] = dot(scores, value_low)
    query_reach[0, 0] = (query * reach).astype(LOW)
    cumulative_out[0, 0] = cumulative
    scores_out[0, 0] = scores


def mix_end_kernel(local, query_reach, incoming, out):
    separated(local[0, 0] + dot(query_reach[0, 0], incoming[0, 0]), out)


def mix_state_grad_kernel(query_reach, grads, out):
    out[0, 0] = dot_tn(query_reach[0, 0], interleaved(grads))


def mix_back_kernel(
    where, f, v, q, lower, starts, starts_row, cumulative_in, scores_in, grads, incoming, next_grad, decay,
    df, dv, dq, lower_grad,
):
    rows = f.shape[3]
    forget_pre, value, query_pre, upstream = interleaved(f), interleaved(v), interleaved(q), interleaved(grads)
    span = forget_pre.shape[0]
    is_start = starts[0].astype(F32) == 1.0
    low_bound = lower[0]
    forget_sig, gate, key, log_decay = gate_terms(forget_pre, low_bound, is_start)
    causal = causal_of(where, span, rows)
    low = causal.astype(LOW)
    cumulative = cumulative_in[0, 0]
    total = jnp.sum(log_decay, axis=0, keepdims=True)
    reach, between, grow, shrink, suffix, _ = decay_terms(causal, starts[0], starts_row[0], cumulative, total)
    query_sig = sigmoid(query_pre)
    query_ext = (query_pre * query_sig * grow).astype(LOW)
    key_shrink = (key * shrink).astype(LOW)
    key_suffix = (key * suffix).astype(LOW)
    value_low = value.astype(LOW)
    state, after_state = incoming[0, 0], next_grad[0, 0]
    grad_scores = (dot_nt(upstream, value_low) * between).astype(LOW)
    grad_ext = dot(grad_scores, key_shrink) + reach * dot_nt(upstream, state)
    grad_shrink = dot_tn(grad_scores, query_ext)
    grad_suffix = dot_nt(value_low, after_state)
    grad_value = dot_tn(scores_in[0, 0], upstream) + dot(key_suffix, after_state)
    suffix_term = key_suffix.astype(F32) * grad_suffix
    terms = query_ext.astype(F32) * grad_ext - key_shrink.astype(F32) * grad_shrink - suffix_term
    ones = jnp.ones((8, HDIM), LOW)
    state_term = thirds(decay[0, 0] * state.astype(F32) * after_state.astype(F32))
    state_row = (dot_nt(ones, state_term[0]) + dot_nt(ones, state_term[1]) + dot_nt(ones, state_term[2]))[:1]
    grad_total = jnp.sum(suffix_term, axis=0, keepdims=True) + state_row
    parts = thirds(terms)
    grad_log = dot_tn(low, parts[0]) + dot_tn(low, parts[1]) + dot_tn(low, parts[2]) + grad_total
    grad_key = grad_shrink * shrink + grad_suffix * suffix
    grad_forget = jnp.where(is_start, 0.0, grad_log / gate) - grad_key
    lower_grad[0, 0] = jnp.broadcast_to(
        jnp.sum(grad_forget * (1.0 - forget_sig), axis=0, keepdims=True), lower_grad.shape[2:]
    )
    separated(grad_forget * (1.0 - low_bound) * forget_sig * (1.0 - forget_sig), df)
    separated(grad_value, dv)
    separated(grad_ext * grow * query_sig * (1.0 + query_pre * (1.0 - query_sig)), dq)


def branch_kernel(plan, names, part, where, tokens, gain_state, gain_ffn, *rest):
    mixed_in, rest = rest[: plan.plane], rest[plan.plane :]
    own, other, mixed, normed_parts, residual, normed_ffn, weight, sems = rest
    here = where[2]
    moves = fetch(
        plan, where,
        [(ref.at[t, u, m], i, j, k, e) for ref, e in ((own, where[3]), (other, where[3] ^ 1)) for t, u, m, i, j, k in names],
        weight, sems,
    )
    for k in range(plan.plane):
        for e in range(plan.nc):
            at = pl.multiple_of(((here ^ k) * plan.nc + e) * part, part)
            mixed[:, pl.ds(at, part)] = mixed_in[k][e].astype(F32)
    values = mixed[...]
    normed = (values * inverse_rms(values) * gain_state[...]).astype(LOW)
    normed_ffn[...] = normed
    for k in range(plan.plane):
        for e in range(plan.nc):
            at = pl.multiple_of(((here ^ k) * plan.nc + e) * part, part)
            normed_parts[k, e] = normed_ffn[:, pl.ds(at, part)]
    for move in moves:
        move.wait()
    total = tokens[...].astype(F32) + dot(normed, weight[...].reshape(-1, weight.shape[-1]))
    residual[...] = total
    normed_ffn[...] = (total * inverse_rms(total) * gain_ffn[...]).astype(LOW)


def branch_back_kernel(
    plan, part, where, upstream, cotangent, residual, mixed, gain_state, gain_ffn, weight,
    grad_residual, branch, grad_parts, scratch,
):
    here = where[2]
    values = residual[...]
    grad = cotangent[...].astype(F32) + norm_back(values, inverse_rms(values), upstream[...] * gain_ffn[...])
    grad_residual[...] = grad
    low = grad.astype(LOW)
    branch[...] = low
    values = mixed[...]
    scaled = dot_nt(low, weight[...].reshape(-1, weight.shape[-1])) * gain_state[...]
    scratch[...] = norm_back(values, inverse_rms(values), scaled).astype(LOW)
    for k in range(plan.plane):
        for e in range(plan.nc):
            at = pl.multiple_of(((here ^ k) * plan.nc + e) * part, part)
            grad_parts[k, e] = scratch[:, pl.ds(at, part)]


def inputs_grad_kernel(df, dv, dq, weight, out):
    part = df.shape[1]
    full = weight[...].reshape(-1, weight.shape[-1])
    out[...] = (
        dot_nt(df[...], full[:, :part]) + dot_nt(dv[...], full[:, part : 2 * part])
        + dot_nt(dq[...], full[:, 2 * part :])
    ).astype(out.dtype)


def body(
    plan, tokens, starts, w_query, w_forget, w_input, w_output, gain_mix, lower_bound, gain_state,
    w_gate, w_up, w_down, gain_ffn, cotangent,
):
    ny, nx, nh, nl, nc, plane, copies = (
        plan.ny, plan.nx, plan.nh, plan.nl, plan.nc, plan.plane, plan.copies
    )
    y, x_, h, l, c = (lax.axis_index(a) for a in AXES)
    here = x_ * nl + l
    where = jnp.stack([y, h, here, c, l * nc, x_]).astype(jnp.int32)
    rows, width = tokens.shape
    r = w_query.shape[0]
    part = width // (plane * nc)
    ffr = w_down.shape[0]
    units = copies * ffr
    heads = part // HDIM
    span = nl * nc * rows
    half = plane * rows
    names = [(i, j) for i in range(nh) for j in range(ny)]

    def fence(*values):
        return lax.optimization_barrier(values)

    def from_plane(blocks):
        return [blocks[0]] + [
            lax.ppermute(blocks[k], ("x", "l"), [(i, i ^ k) for i in range(plane)]) for k in range(1, plane)
        ]

    def swap(x, axis):
        return lax.ppermute(x, axis, [(0, 1), (1, 0)])

    def to_cores(x):
        return lax.all_to_all(x, "chip", 0, 0, tiled=True)

    def turn(x, axis, n):
        return lax.ppermute(x, axis, [(i, (i + 1) % n) for i in range(n)])

    def turns(x, axis, n):
        out = [x]
        for _ in range(1, n):
            out.append(turn(out[-1], axis, n))
        return out

    def over_plane(pieces):
        mine = jnp.concatenate(pieces)
        return to_cores(jnp.stack([mine, mine])).reshape(nc * mine.shape[0], -1)

    def summed_core(x):
        x = to_cores(x.reshape(nc, half, -1)).astype(F32)
        return x[0] + x[1]

    def summed_plane(both):
        both = both.reshape(plane, rows, -1)
        sent = both[1:].astype(LOW)
        got = from_plane([both[0]] + [sent[k] for k in range(plane - 1)])
        return sum((z.astype(F32) for z in got[1:]), got[0])

    def at_plane(x, axis):
        return [lax.dynamic_index_in_dim(x, here ^ k, axis, keepdims=False) for k in range(plane)]

    def collect(sides):
        got = from_plane(
            [lax.dynamic_index_in_dim(sides[k // nl], l ^ (k % nl), 0, keepdims=False) for k in range(plane)]
        )
        return jnp.stack(got, axis=1)

    def to_parts(x):
        return jnp.stack(from_plane([x[k] for k in range(plane)]), axis=1)

    def scatter_y(sent, kept):
        total = sent
        for i, mine in enumerate(kept):
            total = turn(total, "y", ny).astype(F32) + mine.astype(F32)
            total = total.astype(LOW) if i < len(kept) - 1 else total
        return total

    def scatter_h(x):
        def block(i):
            return lax.dynamic_index_in_dim(x, (h - i) % nh, 0, keepdims=False)

        total = block(1 % nh)
        for i in range(2, nh + 1):
            total = turn(total.astype(LOW), "h", nh).astype(F32) + block(i % nh)
        return total

    def rows_of_y(x):
        out = [lax.dynamic_index_in_dim(x, (y - i) % ny, 0, keepdims=False) for i in range(1, ny + 1)]
        return out[0], out[1:]

    small = jnp.concatenate([gain_mix, gain_state, gain_ffn, lower_bound, starts.astype(F32)]).reshape(1, -1)
    small_mine = jnp.concatenate(from_plane([small] * plane))
    small_other = lax.ppermute(small_mine, "chip", [(i, i ^ 1) for i in range(nc)])
    plane_small = jnp.concatenate([pick(c == 0, small_mine, small_other), pick(c == 0, small_other, small_mine)])
    vectors = jnp.concatenate(
        [z for x in turns(plane_small[:, : 4 * r], "h", nh) for z in turns(x, "y", ny)]
    )
    spread = lambda w: w.reshape(r, plane, nc, part)
    three = jnp.concatenate([spread(w_forget), spread(w_input), spread(w_query)], axis=3).transpose(2, 1, 0, 3)
    three = jnp.concatenate(from_plane(at_plane(to_cores(three), 1)))
    down_line = turns(after(w_down, vectors), "h", nh)
    out_first = turns(w_output, "y", ny)
    tokens_pair = jnp.concatenate([tokens, swap(after(tokens, three), "l")])
    cotangent_x = swap(after(cotangent, three), "x")
    (packed,) = call(partial(pack_kernel, plan, ffr), [shape((nc, plane, r, 2 * units), LOW)], w_gate, w_up)
    packed = to_cores(packed)
    plane_small, vectors, three, down_line, out_first, tokens_pair, cotangent_x, packed, w_output = fence(
        plane_small, vectors, three, down_line, out_first, tokens_pair, cotangent_x, packed, w_output
    )

    three_line = turns(three, "h", nh)
    three_first = turns(three, "y", ny)
    out_line = turns(after(w_output, three_line), "h", nh)
    tokens_far = swap(tokens_pair, "x")
    cotangent_l = swap(jnp.concatenate([cotangent, cotangent_x]), "l")
    gate_up = from_plane(after(at_plane(packed, 1), tokens_far, cotangent_l))
    gate_up = [jnp.concatenate(gate_up[:nl]), jnp.concatenate(gate_up[nl:])]
    three_line, three_first, out_line, tokens_pair, tokens_far, cotangent_l, gate_up, down_line = fence(
        three_line, three_first, out_line, tokens_pair, tokens_far, cotangent_l, gate_up, down_line
    )

    three = three_first + [z for x in three_line[1:] for z in turns(x, "y", ny)]
    out_copies = out_first + [z for x in out_line[1:] for z in turns(x, "y", ny)]
    gu_first = jnp.stack(turns(gate_up[0], "h", nh))
    plane_tokens = over_plane([tokens_pair, tokens_far])
    plane_starts = (
        plane_small[:, 4 * r :].reshape(nc, nx, nl, rows).transpose(1, 2, 0, 3).reshape(nx, span)
    )
    starts_row = jnp.broadcast_to(plane_starts[:, None], (nx, 8, span)).astype(LOW)
    starts_wide = jnp.broadcast_to(plane_starts[:, :, None], (nx, span, HDIM)).astype(LOW)
    places = jnp.stack([
        plan.owner((y - j) % ny, here ^ k, (h - i) % nh, e)
        for i, j in names for e in range(nc) for k in range(plane)
    ])
    ordered = (jnp.arange(plan.devices)[:, None] == places[None, :]).astype(F32)
    vectors = jnp.dot(ordered, vectors, precision=lax.Precision.HIGHEST)
    vectors = vectors.reshape(plan.devices, 4, r).transpose(1, 0, 2).reshape(4, width)
    full_gain_mix, full_gain_state, full_gain_ffn = (vectors[i : i + 1] for i in range(3))
    lower = lax.dynamic_slice_in_dim(vectors[3], (here * nc + c) * part, part).reshape(heads, 1, HDIM)
    count = plan.devices
    total = nc * half
    project_flops = 2 * total * width * 3 * part
    normed_in, pre, w_three = call(
        partial(project_kernel, plan, names),
        [shape((total, width), LOW), shape((total, 3 * part)), shape((count, r, 3 * part), LOW)],
        where, plane_tokens, full_gain_mix, *three,
        specs=[SMEM, VMEM, VMEM] + [ANY] * copies,
        scratch=[pltpu.SemaphoreType.DMA((count,))],
        flops=project_flops,
    )
    down_line, gate_up, pre, out_copies, lower, starts_wide, starts_row, gu_first = fence(
        down_line, gate_up, pre, out_copies, lower, starts_wide, starts_row, gu_first
    )

    by_group = lambda x: x.reshape(nc, nx, nl, rows, -1)
    piece = lambda i: pl.BlockSpec((nc, 1, nl, rows, HDIM), lambda g, a, i=i: (0, g, 0, 0, i * heads + a))
    state_spec = pl.BlockSpec((1, 1, HDIM, HDIM), lambda g, a: (g, a, 0, 0))
    rows_spec = pl.BlockSpec((1, 1, span, HDIM), lambda g, a: (g, a, 0, 0))
    scores_spec = pl.BlockSpec((1, 1, span, span), lambda g, a: (g, a, 0, 0))
    head_spec = pl.BlockSpec((1, 1, HDIM), lambda g, a: (a, 0, 0))
    starts_spec = pl.BlockSpec((1, span, HDIM), lambda g, a: (g, 0, 0))
    starts_row_spec = pl.BlockSpec((1, 8, span), lambda g, a: (g, 0, 0))
    pre_args = (by_group(pre),) * 3
    pre_specs = [piece(0), piece(1), piece(2)]
    states = (nx, heads, HDIM, HDIM)
    by_row = (nx, heads, span, HDIM)
    grouped = (nc, nx, nl, rows, part)
    mix_flops = nx * heads * 2 * span * span * HDIM
    end_state, decay, local, query_reach, cumulative, scores = call(
        mix_kernel,
        [shape(states), shape(states), shape(by_row), shape(by_row, LOW), shape(by_row),
         shape((nx, heads, span, span), LOW)],
        where, *pre_args, lower, starts_wide, starts_row,
        grid=(nx, heads),
        specs=[SMEM] + pre_specs + [head_spec, starts_spec, starts_row_spec],
        out_specs=[state_spec, state_spec, rows_spec, rows_spec, rows_spec, scores_spec],
        flops=8 * mix_flops,
    )
    down_blocks = turns(jnp.stack(down_line), "y", ny)
    gu_second = jnp.stack(turns(gate_up[1], "h", nh))
    cut = copies // 2
    pieces = [jnp.stack(out_copies[:cut]), jnp.stack(out_copies[cut:])]
    moved = [swap(z, axis) for z, axis in zip(pieces, ("l", "x"))]
    pairs = [jnp.stack([a, z]) for a, z in zip(pieces, moved)]
    moved = [swap(z, axis) for z, axis in zip(pairs, ("x", "l"))]
    groups = jnp.stack([pairs[0], moved[0], pairs[1], moved[1]])
    out_names = [
        (t * 2 + distance, u, m, *names[t * cut + m], u * nl + distance if t else distance * nl + u)
        for t in range(2) for distance in range(2) for u in range(2) for m in range(cut)
    ]
    end_state, decay, local, query_reach, down_blocks, gu_first, groups, gu_second = fence(
        end_state, decay, local, query_reach, down_blocks, gu_first, groups, gu_second
    )

    def carry(block, step):
        incoming = jnp.zeros_like(block)
        for t in range(nh - 1):
            pairs = [(i, i + step) for i in range(nh) if 0 <= i + step < nh]
            sent = decay * incoming + block if t else block
            incoming = lax.ppermute(sent.astype(LOW), "h", pairs)
            incoming = incoming if t == nh - 2 else incoming.astype(F32)
        return incoming

    incoming = carry(end_state, 1)
    (mixed,) = call(
        mix_end_kernel, [shape(grouped, LOW)], local, query_reach, incoming,
        grid=(nx, heads), specs=[rows_spec, rows_spec, state_spec], out_specs=[piece(0)], flops=mix_flops // 4,
    )
    mixed = to_cores(mixed.reshape(nc, plane, rows, part))
    mixed_in = from_plane([mixed[:, k] for k in range(plane)])
    gu_first = turns(gu_first, "y", ny)
    groups_other = lax.ppermute(groups, "chip", [(i, i ^ 1) for i in range(nc)])
    mixed_in, gu_first, groups, groups_other, down_blocks, gu_second = fence(
        mixed_in, gu_first, groups, groups_other, down_blocks, gu_second
    )

    parts_shape = (plane, nc, rows, part)
    mixed, normed_parts, residual, normed_ffn, w_out_full = call(
        partial(branch_kernel, plan, out_names, part),
        [shape((rows, width)), shape(parts_shape, LOW), shape((rows, width)), shape((rows, width), LOW),
         shape((count, r, width), LOW)],
        where, tokens, full_gain_state, full_gain_ffn, *mixed_in, groups, groups_other,
        specs=[SMEM] + [VMEM] * (3 + plane) + [ANY] * 2,
        scratch=[pltpu.SemaphoreType.DMA((count,))],
        flops=2 * rows * width * width,
    )
    ffn_pieces = from_plane([normed_ffn] * plane)
    gate_up = gu_first + turns(gu_second, "y", ny)
    plane_cotangent = over_plane([cotangent, cotangent_l[:rows], cotangent_x, cotangent_l[rows:]])
    down = jnp.zeros((ny, nh, ffr, width), LOW)
    for j, blocks in enumerate(down_blocks):
        for i in range(nh):
            down = lax.dynamic_update_slice(down, blocks[i][None, None], ((y - j) % ny, (h - i) % nh, 0, 0))
    down = down.reshape(units, width)
    ffn_pieces, gate_up, down, normed_parts, plane_cotangent = fence(
        ffn_pieces, gate_up, down, normed_parts, plane_cotangent
    )

    plane_ffn = over_plane(ffn_pieces)
    gu_names = [(j, k) for k in (0, nl) for j in range(ny)]
    step = min(256, half)
    row_spec = lambda n: pl.BlockSpec((step, n), lambda t: (t, 0))
    hidden, grad_gu, part_out, part_ffn = call(
        partial(ffn_kernel, plan, gu_names),
        [shape((total, units), LOW), shape((total, 2 * units), LOW), shape((total, width), LOW),
         shape((total, width), LOW)],
        where, plane_ffn, plane_cotangent, down, *gate_up,
        grid=(total // step,),
        specs=[SMEM, row_spec(width), row_spec(width), VMEM] + [ANY] * len(gate_up),
        out_specs=[row_spec(units), row_spec(2 * units), row_spec(width), row_spec(width)],
        scratch=[pltpu.VMEM((count, r, 2 * units), LOW), pltpu.SemaphoreType.DMA((count,))],
        flops=2 * total * width * units * 7,
    )
    mix_parts = to_parts(normed_parts)
    lcr = nl * nc * r

    def columns_grad(turns, dtype, sides, normed, grads):
        n = sum(g.shape[1] for g in grads)
        return call(
            partial(columns_grad_kernel, plan, turns, sides, len(grads)), [shape((nh, len(sides), lcr, n), dtype)],
            where, normed, *grads, specs=[SMEM] + [VMEM] * (1 + len(grads)),
            flops=2 * total * width * n * len(sides) // (ny * nx),
        )[0]

    def columns_kept(sides, *arrays):
        return [columns_grad(i % ny, F32 if i == ny else LOW, sides, *arrays) for i in range(2, ny + 1)]

    both_ffn = summed_core(part_ffn)
    far_sent = columns_grad(1, LOW, (1,), plane_ffn, [grad_gu])
    both_ffn, far_sent, plane_ffn, grad_gu, hidden, mix_parts, plane_cotangent, part_out = fence(
        both_ffn, far_sent, plane_ffn, grad_gu, hidden, mix_parts, plane_cotangent, part_out
    )

    grad_normed_ffn = summed_plane(both_ffn)
    near_sent = columns_grad(1, LOW, (0,), plane_ffn, [grad_gu])
    grad_gu_far = scatter_y(far_sent, columns_kept((1,), plane_ffn, [grad_gu]))
    (grad_down,) = call(
        rows_grad_kernel, [shape((units, width), LOW)], hidden, plane_cotangent, flops=2 * total * units * width,
    )
    both_out = summed_core(after(part_out, near_sent))
    grad_gu_far, grad_normed_ffn, near_sent, grad_down, plane_ffn, grad_gu, both_out = fence(
        grad_gu_far, grad_normed_ffn, near_sent, grad_down, plane_ffn, grad_gu, both_out
    )

    grad_gu_near = scatter_y(near_sent, columns_kept((0,), plane_ffn, [grad_gu]))
    grad_residual, branch, grad_parts = call(
        partial(branch_back_kernel, plan, part),
        [shape((rows, width)), shape((rows, width), LOW), shape(parts_shape, LOW)],
        where, grad_normed_ffn, cotangent, residual, mixed, full_gain_state, full_gain_ffn, w_out_full,
        specs=[SMEM] + [VMEM] * 7,
        scratch=[pltpu.VMEM((rows, width), LOW)],
        flops=2 * rows * width * width,
    )
    grads = to_parts(grad_parts)
    branch_pieces = from_plane([after(branch, grads)] * plane)
    grad_gu_far = scatter_h(grad_gu_far)
    grads = by_group(to_cores(grads))
    (state_grad,) = call(
        mix_state_grad_kernel, [shape(states)], query_reach, grads,
        grid=(nx, heads), specs=[rows_spec, piece(0)], out_specs=[state_spec], flops=mix_flops // 4,
    )
    mix_parts = to_cores(mix_parts)
    grad_gu_near, state_grad, grads, branch_pieces, grad_gu_far, grad_down, both_out, mix_parts = fence(
        grad_gu_near, state_grad, grads, branch_pieces, grad_gu_far, grad_down, both_out, mix_parts
    )

    next_grad = carry(state_grad, -1)
    output = (residual + summed_plane(both_out)).astype(LOW)
    grad_down = scatter_y(*rows_of_y(grad_down.reshape(ny, nh, ffr, width)))
    df, dv, dq, lower_grad = call(
        mix_back_kernel,
        [shape(grouped, LOW)] * 3 + [shape((nx, heads, 8, HDIM))],
        where, *pre_args, lower, starts_wide, starts_row, cumulative, scores, grads, incoming, next_grad, decay,
        grid=(nx, heads),
        specs=[SMEM] + pre_specs + [head_spec, starts_spec, starts_row_spec, rows_spec, scores_spec]
        + [piece(0), state_spec, state_spec, state_spec],
        out_specs=[piece(0)] * 3 + [pl.BlockSpec((1, 1, 8, HDIM), lambda g, a: (g, a, 0, 0))],
        flops=12 * mix_flops,
    )
    pre_grads = [g.reshape(total, part) for g in (df, dv, dq)]
    (part_in,) = call(
        inputs_grad_kernel, [shape((total, width), LOW)], *pre_grads, w_three, flops=project_flops
    )
    both_in = summed_core(part_in)
    three_sent = columns_grad(1, LOW, (0, 1), normed_in, pre_grads)
    both_in, three_sent, pre_grads, branch_pieces, grad_down, grad_gu_near, output = fence(
        both_in, three_sent, pre_grads, branch_pieces, grad_down, grad_gu_near, output
    )

    grad_normed_in = summed_plane(both_in)
    grad_three = scatter_y(three_sent, columns_kept((0, 1), normed_in, pre_grads))
    grad_gu_near = scatter_h(grad_gu_near)
    (grad_out,) = call(
        rows_grad_kernel, [shape((part, width), LOW)], mix_parts.reshape(total, part), over_plane(branch_pieces),
        flops=2 * total * part * width,
    )
    grad_three, grad_normed_in, grad_gu_near, grad_out, grad_down, grad_gu_far = fence(
        grad_three, grad_normed_in, grad_gu_near, grad_out, grad_down, grad_gu_far
    )

    own_tokens = tokens.astype(F32)
    grad_tokens = grad_residual + norm_back(own_tokens, inverse_rms(own_tokens), grad_normed_in * full_gain_mix)
    grad_three = scatter_h(grad_three).astype(LOW).reshape(nx, nl, nc, r, 3 * part)
    grad_output = scatter_y(*rows_of_y(grad_out.reshape(ny, nh, r, width)))
    gu_blocks = collect([z.astype(LOW).reshape(nl, nc, r, 2 * units) for z in (grad_gu_near, grad_gu_far)])
    lower_grad = jnp.sum(lower_grad[:, :, 0], axis=0).reshape(1, part)
    lower_grad = sum(turns(lower_grad, "y", ny))
    grad_three, grad_output, gu_blocks, lower_grad, grad_down = fence(
        grad_three, grad_output, gu_blocks, lower_grad, grad_down
    )

    three_blocks = collect([grad_three[t] for t in range(nx)])
    grad_output = scatter_h(grad_output)
    lower_grad = sum(turns(lower_grad, "h", nh))
    grad_down = scatter_h(after(grad_down, lower_grad))
    owners = []
    for j in range(ny):
        for p in range(nx):
            for i in range(nh):
                for o in range(nl):
                    for e in range(nc):
                        owners.append(((p * nl + o) * nc + e) * copies + j * nh + i)
    pairs = list(enumerate(owners))
    along = shape((r, HDIM))
    grad_w_gate, grad_w_up, along_ffn = call(
        partial(unpack_kernel, plan, ffr), [shape(w_gate.shape), shape(w_up.shape), along],
        where, to_cores(gu_blocks), w_gate, w_up, specs=[SMEM] + [VMEM] * 3,
        scratch=[pltpu.VMEM((nc, plane, r, 2 * units), LOW)],
    )
    grad_w_forget, grad_w_input, grad_w_query, along_mix = call(
        partial(unpack_part_kernel, plan, part), [shape(w_query.shape)] * 3 + [along],
        where, to_cores(three_blocks), w_forget, w_input, w_query, specs=[SMEM] + [VMEM] * 4,
    )
    grad_output = lax.ppermute(grad_output.astype(LOW), AXES, pairs).astype(F32)
    lower_grad = lax.dynamic_index_in_dim(lower_grad.reshape(copies, r), y * nh + h, 0, keepdims=False)
    lower_grad = lax.ppermute(lower_grad, AXES, pairs)
    grad_gain_mix = along_mix[:, 0] / gain_mix
    grad_gain_ffn = along_ffn[:, 0] / gain_ffn
    grad_gain_state = jnp.sum(w_output.astype(F32) * grad_output, axis=1) / gain_state
    return (
        output, grad_tokens, grad_w_query, grad_w_forget, grad_w_input, grad_output, grad_gain_mix, lower_grad,
        grad_gain_state, grad_w_gate, grad_w_up, grad_down, grad_gain_ffn,
    )


def solution(mesh):
    nb, ns, nc = (mesh.shape[a] for a in ("batch", "seq", "chip"))
    sizes = (nb // 2, 2, ns // 2, 2, nc)
    fine = jax.sharding.Mesh(mesh.devices.reshape(sizes), AXES)
    flat, matrix = P(AXES), P(AXES, None)
    return jax.shard_map(
        partial(body, Plan(sizes)),
        mesh=fine,
        in_specs=(
            matrix, flat, matrix, matrix, matrix, matrix, flat, flat, flat, matrix, matrix, matrix, flat, matrix,
        ),
        out_specs=(
            matrix, matrix, matrix, matrix, matrix, matrix, flat, flat, flat, matrix, matrix, matrix, flat,
        ),
        check_vma=False,
    )
```

```python
import math
from functools import partial

import jax
import jax.numpy as jnp
from jax import lax
from jax.experimental import pallas as pl
from jax.experimental.pallas import tpu as pltpu
from jax.sharding import PartitionSpec as P

HDIM = 128
EPSILON = 1e-06
RESET_LOG = -30.0
F32 = jnp.float32
LOW = jnp.bfloat16
AXES = ("y", "x", "h", "l", "chip")
LIMIT = 56 * 2**20
VMEM = pl.BlockSpec(memory_space=pltpu.VMEM)
SMEM = pl.BlockSpec(memory_space=pltpu.SMEM)
ANY = pl.BlockSpec(memory_space=pl.ANY)


def dot(left, right):
    return jnp.dot(left, right, preferred_element_type=F32)


def dot_tn(left, right):
    return lax.dot_general(left, right, (((0,), (0,)), ((), ())), preferred_element_type=F32)


def dot_nt(left, right):
    return lax.dot_general(left, right, (((1,), (1,)), ((), ())), preferred_element_type=F32)


def inverse_rms(values):
    return lax.rsqrt(jnp.mean(values * values, axis=-1, keepdims=True) + EPSILON)


def norm_back(values, rms, scaled):
    inner = jnp.mean(scaled * values, axis=-1, keepdims=True)
    return rms * scaled - values * (rms * rms * rms * inner)


def sigmoid(a):
    return 1.0 / (1.0 + jnp.exp(-a))


def pick(flag, first, second):
    return jnp.where(flag, first, second)


def after(x, *deps):
    return lax.optimization_barrier((x, deps))[0]


def shape(dims, dtype=F32):
    return jax.ShapeDtypeStruct(tuple(dims), dtype)


def call(kernel, outs, *args, specs=None, out_specs=None, grid=(), scratch=(), flops=0):
    outs = tuple(outs)
    specs = [VMEM] * len(args) if specs is None else specs
    out_specs = tuple([VMEM] * len(outs)) if out_specs is None else tuple(out_specs)
    moved = sum(math.prod(a.shape) * a.dtype.itemsize for a in (*args, *outs))
    return pl.pallas_call(
        kernel,
        out_shape=outs,
        grid=grid,
        in_specs=specs,
        out_specs=out_specs,
        scratch_shapes=list(scratch),
        compiler_params=pltpu.CompilerParams(vmem_limit_bytes=LIMIT),
        cost_estimate=pl.CostEstimate(flops=int(flops) // 8, bytes_accessed=int(moved) // 8, transcendentals=0),
    )(*args)


class Plan:
    def __init__(self, sizes):
        self.ny, self.nx, self.nh, self.nl, self.nc = sizes
        self.plane = self.nx * self.nl
        self.copies = self.ny * self.nh
        self.devices = self.copies * self.plane * self.nc

    def owner(self, y, p, h, c):
        return (((y * self.nx + p // self.nl) * self.nh + h) * self.nl + p % self.nl) * self.nc + c


def fetch(plan, where, blocks, target, sems, start=True):
    y, h, here = (where[i] for i in range(3))
    moves = []
    for t, (source, i, j, k, e) in enumerate(blocks):
        yy = lax.rem(y + (plan.ny - j), plan.ny)
        hh = lax.rem(h + (plan.nh - i), plan.nh)
        place = plan.owner(yy, here ^ k, hh, e)
        move = pltpu.make_async_copy(source, target.at[place], sems.at[t])
        if start:
            move.start()
        moves.append(move)
    return moves


def pack_kernel(plan, ffr, gate, up, out):
    units = plan.copies * ffr
    for e in range(plan.nc):
        for p in range(plan.plane):
            for w, base in ((gate, 0), (up, units)):
                for m in range(plan.copies):
                    at = plan.owner(m // plan.nh, p, m % plan.nh, e) * ffr
                    to = base + m * ffr
                    out[e, p, :, to : to + ffr] = w[:, at : at + ffr]


def unpack_kernel(plan, ffr, where, blocks, gate, up, grad_gate, grad_up, along, ordered):
    here = where[2]
    units = plan.copies * ffr
    for k in range(plan.plane):
        for e in range(plan.nc):
            ordered[e, here ^ k] = blocks[e, k]
    for e in range(plan.nc):
        for p in range(plan.plane):
            block = ordered[e, p].astype(F32)
            for g, base in ((grad_gate, 0), (grad_up, units)):
                for m in range(plan.copies):
                    at = plan.owner(m // plan.nh, p, m % plan.nh, e) * ffr
                    to = base + m * ffr
                    g[:, at : at + ffr] = block[:, to : to + ffr]
    total = jnp.sum(gate[...].astype(F32) * grad_gate[...], axis=1, keepdims=True)
    total = total + jnp.sum(up[...].astype(F32) * grad_up[...], axis=1, keepdims=True)
    along[...] = jnp.broadcast_to(total, along.shape)


def unpack_part_kernel(plan, part, where, blocks, w0, w1, w2, g0, g1, g2, along):
    here = where[2]
    for k in range(plan.plane):
        for e in range(plan.nc):
            at = pl.multiple_of(((here ^ k) * plan.nc + e) * part, part)
            for i, g in enumerate((g0, g1, g2)):
                g[:, pl.ds(at, part)] = blocks[e, k, :, i * part : (i + 1) * part].astype(F32)
    total = 0.0
    for w, g in ((w0, g0), (w1, g1), (w2, g2)):
        total = total + jnp.sum(w[...].astype(F32) * g[...], axis=1, keepdims=True)
    along[...] = jnp.broadcast_to(total, along.shape)


def normalize(x, gain, out, step):
    @pl.loop(0, x.shape[0] // step)
    def _(t):
        at = pl.ds(pl.multiple_of(t * step, step), step)
        values = x[at, :].astype(F32)
        out[at, :] = (values * inverse_rms(values) * gain[...]).astype(LOW)


def project_kernel(plan, names, where, x, gain, *rest):
    blocks, (normed, pre, weight, sems) = rest[: len(names)], rest[len(names) :]
    moves = fetch(
        plan, where,
        [(ref.at[k * plan.nc + e], i, j, k, e) for ref, (i, j) in zip(blocks, names)
         for k in range(plan.plane) for e in range(plan.nc)],
        weight, sems,
    )
    normalize(x, gain, normed, 64)
    for move in moves:
        move.wait()
    pre[...] = dot(normed[...], weight[...].reshape(-1, weight.shape[-1]))


def ffn_kernel(plan, names, where, normed, cotangent, down, *rest):
    blocks, (hidden, grad_gu, part_out, part_grad, weight, sems) = rest[: len(names)], rest[len(names) :]
    first = pl.program_id(0) == 0

    def moves(start):
        return fetch(
            plan, where,
            [(ref.at[i, k * plan.nc + e], i, j, base + k, e) for ref, (j, base) in zip(blocks, names)
             for i in range(plan.nh) for k in range(ref.shape[1] // plan.nc) for e in range(plan.nc)],
            weight, sems, start,
        )

    @pl.when(first)
    def _():
        moves(True)

    units = down.shape[0]
    upstream = dot_nt(cotangent[...], down[...])

    @pl.when(first)
    def _():
        for move in moves(False):
            move.wait()

    full = weight[...].reshape(-1, weight.shape[-1])
    both = dot(normed[...], full)
    gate, up = both[:, :units], both[:, units:]
    sig = sigmoid(gate)
    silu = gate * sig
    hid = (silu * up).astype(LOW)
    hidden[...] = hid
    grad_gu[:, :units] = (upstream * up * sig * (1.0 + gate * (1.0 - sig))).astype(LOW)
    grad_gu[:, units:] = (upstream * silu).astype(LOW)
    part_grad[...] = dot_nt(grad_gu[...], full).astype(part_grad.dtype)
    part_out[...] = dot(hid, down[...]).astype(part_out.dtype)


def columns_grad_kernel(plan, turn, sides, count, where, normed, *rest):
    grads, out = rest[:count], rest[count]
    y = lax.rem(where[0] + (plan.ny - turn), plan.ny)
    step = out.shape[0] * out.shape[2]
    for t, side in enumerate(sides):
        at = pl.multiple_of((y * plan.nx + (where[5] ^ side)) * step, step)
        base = 0
        for a in grads:
            n = a.shape[1]
            value = dot_tn(normed[:, pl.ds(at, step)], a[...])
            for i in range(plan.nh):
                out[i, t, :, base : base + n] = value[i * out.shape[2] : (i + 1) * out.shape[2]].astype(out.dtype)
            base += n


def rows_grad_kernel(left, right, out):
    n = 512
    for t in range(out.shape[1] // n):
        at = slice(t * n, (t + 1) * n)
        out[:, at] = dot_tn(left[...], right[:, at]).astype(out.dtype)


def interleaved(x):
    return jnp.concatenate([x[e, 0, i] for i in range(x.shape[2]) for e in range(x.shape[0])], axis=0)


def separated(x, out):
    nc, _, nl, rows, _ = out.shape
    for i in range(nl):
        for e in range(nc):
            at = (i * nc + e) * rows
            out[e, 0, i] = x[at : at + rows].astype(out.dtype)


def thirds(x):
    first = x.astype(LOW)
    rest = x - first.astype(F32)
    second = rest.astype(LOW)
    return first, second, (rest - second.astype(F32)).astype(LOW)


def causal_of(where, span, rows):
    flip = where[4] * rows
    t = lax.broadcasted_iota(jnp.int32, (span, span), 0) ^ flip
    s = lax.broadcasted_iota(jnp.int32, (span, span), 1) ^ flip
    return (t >= s).astype(F32)


def gate_terms(forget_pre, lower, is_start):
    sig = sigmoid(forget_pre)
    gate = lower + (1.0 - lower) * sig
    return sig, gate, 1.0 - gate, jnp.where(is_start, 0.0, jnp.log(gate))


def decay_terms(causal, starts, starts_row, cumulative, total):
    low = causal.astype(LOW)
    count = dot(low, starts)
    count_row = dot_nt(starts_row, low)[:1]
    ends = jnp.sum(starts.astype(F32), axis=0, keepdims=True)
    reach = jnp.exp(RESET_LOG * count)
    left = jnp.exp(RESET_LOG * (ends - count))
    between = causal * jnp.exp(RESET_LOG * jnp.maximum(count[:, :1] - count_row, 0.0))
    return reach, between, jnp.exp(cumulative), jnp.exp(-cumulative), jnp.exp(total - cumulative) * left, ends


def mix_kernel(
    where, f, v, q, lower, starts, starts_row,
    end_state, decay, local, query_reach, cumulative_out, scores_out,
):
    rows = f.shape[3]
    forget_pre, value, query_pre = interleaved(f), interleaved(v), interleaved(q)
    span = forget_pre.shape[0]
    is_start = starts[0].astype(F32) == 1.0
    _, _, key, log_decay = gate_terms(forget_pre, lower[0], is_start)
    causal = causal_of(where, span, rows)
    low = causal.astype(LOW)
    parts = thirds(log_decay)
    cumulative = dot(low, parts[0]) + dot(low, parts[1]) + dot(low, parts[2])
    total = jnp.sum(log_decay, axis=0, keepdims=True)
    reach, between, grow, shrink, suffix, ends = decay_terms(causal, starts[0], starts_row[0], cumulative, total)
    query = query_pre * sigmoid(query_pre) * grow
    value_low = value.astype(LOW)
    end_state[0, 0] = dot_tn((key * suffix).astype(LOW), value_low)
    ones = jnp.ones((span, HDIM), LOW)
    total_column = dot_tn(parts[0], ones) + dot_tn(parts[1], ones) + dot_tn(parts[2], ones)
    decay[0, 0] = jnp.exp(total_column + RESET_LOG * ends)
    scores = (dot_nt(query.astype(LOW), (key * shrink).astype(LOW)) * between).astype(LOW)
    local[0, 0] = dot(scores, value_low)
    query_reach[0, 0] = (query * reach).astype(LOW)
    cumulative_out[0, 0] = cumulative
    scores_out[0, 0] = scores


def mix_end_kernel(local, query_reach, incoming, out):
    separated(local[0, 0] + dot(query_reach[0, 0], incoming[0, 0]), out)


def mix_state_grad_kernel(query_reach, grads, out):
    out[0, 0] = dot_tn(query_reach[0, 0], interleaved(grads))


def mix_back_kernel(
    where, f, v, q, lower, starts, starts_row, cumulative_in, scores_in, grads, incoming, next_grad, decay,
    df, dv, dq, lower_grad,
):
    rows = f.shape[3]
    forget_pre, value, query_pre, upstream = interleaved(f), interleaved(v), interleaved(q), interleaved(grads)
    span = forget_pre.shape[0]
    is_start = starts[0].astype(F32) == 1.0
    low_bound = lower[0]
    forget_sig, gate, key, log_decay = gate_terms(forget_pre, low_bound, is_start)
    causal = causal_of(where, span, rows)
    low = causal.astype(LOW)
    cumulative = cumulative_in[0, 0]
    total = jnp.sum(log_decay, axis=0, keepdims=True)
    reach, between, grow, shrink, suffix, _ = decay_terms(causal, starts[0], starts_row[0], cumulative, total)
    query_sig = sigmoid(query_pre)
    query_ext = (query_pre * query_sig * grow).astype(LOW)
    key_shrink = (key * shrink).astype(LOW)
    key_suffix = (key * suffix).astype(LOW)
    value_low = value.astype(LOW)
    state, after_state = incoming[0, 0], next_grad[0, 0]
    grad_scores = (dot_nt(upstream, value_low) * between).astype(LOW)
    grad_ext = dot(grad_scores, key_shrink) + reach * dot_nt(upstream, state)
    grad_shrink = dot_tn(grad_scores, query_ext)
    grad_suffix = dot_nt(value_low, after_state)
    grad_value = dot_tn(scores_in[0, 0], upstream) + dot(key_suffix, after_state)
    suffix_term = key_suffix.astype(F32) * grad_suffix
    terms = query_ext.astype(F32) * grad_ext - key_shrink.astype(F32) * grad_shrink - suffix_term
    ones = jnp.ones((8, HDIM), LOW)
    state_term = thirds(decay[0, 0] * state.astype(F32) * after_state.astype(F32))
    state_row = (dot_nt(ones, state_term[0]) + dot_nt(ones, state_term[1]) + dot_nt(ones, state_term[2]))[:1]
    grad_total = jnp.sum(suffix_term, axis=0, keepdims=True) + state_row
    parts = thirds(terms)
    grad_log = dot_tn(low, parts[0]) + dot_tn(low, parts[1]) + dot_tn(low, parts[2]) + grad_total
    grad_key = grad_shrink * shrink + grad_suffix * suffix
    grad_forget = jnp.where(is_start, 0.0, grad_log / gate) - grad_key
    lower_grad[0, 0] = jnp.broadcast_to(
        jnp.sum(grad_forget * (1.0 - forget_sig), axis=0, keepdims=True), lower_grad.shape[2:]
    )
    separated(grad_forget * (1.0 - low_bound) * forget_sig * (1.0 - forget_sig), df)
    separated(grad_value, dv)
    separated(grad_ext * grow * query_sig * (1.0 + query_pre * (1.0 - query_sig)), dq)


def branch_kernel(plan, names, part, where, tokens, gain_state, gain_ffn, *rest):
    mixed_in, rest = rest[: plan.plane], rest[plan.plane :]
    own, other, mixed, normed_parts, residual, normed_ffn, weight, sems = rest
    here = where[2]
    moves = fetch(
        plan, where,
        [(ref.at[t, u, m], i, j, k, e) for ref, e in ((own, where[3]), (other, where[3] ^ 1)) for t, u, m, i, j, k in names],
        weight, sems,
    )
    for k in range(plan.plane):
        for e in range(plan.nc):
            at = pl.multiple_of(((here ^ k) * plan.nc + e) * part, part)
            mixed[:, pl.ds(at, part)] = mixed_in[k][e].astype(F32)
    values = mixed[...]
    normed = (values * inverse_rms(values) * gain_state[...]).astype(LOW)
    normed_ffn[...] = normed
    for k in range(plan.plane):
        for e in range(plan.nc):
            at = pl.multiple_of(((here ^ k) * plan.nc + e) * part, part)
            normed_parts[k, e] = normed_ffn[:, pl.ds(at, part)]
    for move in moves:
        move.wait()
    total = tokens[...].astype(F32) + dot(normed, weight[...].reshape(-1, weight.shape[-1]))
    residual[...] = total
    normed_ffn[...] = (total * inverse_rms(total) * gain_ffn[...]).astype(LOW)


def branch_back_kernel(
    plan, part, where, upstream, cotangent, residual, mixed, gain_state, gain_ffn, weight,
    grad_residual, branch, grad_parts, scratch,
):
    here = where[2]
    values = residual[...]
    grad = cotangent[...].astype(F32) + norm_back(values, inverse_rms(values), upstream[...] * gain_ffn[...])
    grad_residual[...] = grad
    low = grad.astype(LOW)
    branch[...] = low
    values = mixed[...]
    scaled = dot_nt(low, weight[...].reshape(-1, weight.shape[-1])) * gain_state[...]
    scratch[...] = norm_back(values, inverse_rms(values), scaled).astype(LOW)
    for k in range(plan.plane):
        for e in range(plan.nc):
            at = pl.multiple_of(((here ^ k) * plan.nc + e) * part, part)
            grad_parts[k, e] = scratch[:, pl.ds(at, part)]


def inputs_grad_kernel(df, dv, dq, weight, out):
    part = df.shape[1]
    full = weight[...].reshape(-1, weight.shape[-1])
    out[...] = (
        dot_nt(df[...], full[:, :part]) + dot_nt(dv[...], full[:, part : 2 * part])
        + dot_nt(dq[...], full[:, 2 * part :])
    ).astype(out.dtype)


def body(
    plan, tokens, starts, w_query, w_forget, w_input, w_output, gain_mix, lower_bound, gain_state,
    w_gate, w_up, w_down, gain_ffn, cotangent,
):
    ny, nx, nh, nl, nc, plane, copies = (
        plan.ny, plan.nx, plan.nh, plan.nl, plan.nc, plan.plane, plan.copies
    )
    y, x_, h, l, c = (lax.axis_index(a) for a in AXES)
    here = x_ * nl + l
    where = jnp.stack([y, h, here, c, l * nc, x_]).astype(jnp.int32)
    rows, width = tokens.shape
    r = w_query.shape[0]
    part = width // (plane * nc)
    ffr = w_down.shape[0]
    units = copies * ffr
    heads = part // HDIM
    span = nl * nc * rows
    half = plane * rows
    names = [(i, j) for i in range(nh) for j in range(ny)]

    def fence(*values):
        return lax.optimization_barrier(values)

    def from_plane(blocks):
        return [blocks[0]] + [
            lax.ppermute(blocks[k], ("x", "l"), [(i, i ^ k) for i in range(plane)]) for k in range(1, plane)
        ]

    def swap(x, axis):
        return lax.ppermute(x, axis, [(0, 1), (1, 0)])

    def to_cores(x):
        return lax.all_to_all(x, "chip", 0, 0, tiled=True)

    def turn(x, axis, n):
        return lax.ppermute(x, axis, [(i, (i + 1) % n) for i in range(n)])

    def turns(x, axis, n):
        out = [x]
        for _ in range(1, n):
            out.append(turn(out[-1], axis, n))
        return out

    def over_plane(pieces):
        mine = jnp.concatenate(pieces)
        return to_cores(jnp.stack([mine, mine])).reshape(nc * mine.shape[0], -1)

    def summed_core(x):
        x = to_cores(x.reshape(nc, plane, rows, -1))
        sums = [x[0, k].astype(F32) + x[1, k].astype(F32) for k in range(plane)]
        return [sums[0]] + [z.astype(LOW) for z in sums[1:]]

    def summed_plane(sums):
        got = from_plane(sums)
        return sum((z.astype(F32) for z in got[1:]), got[0])

    def at_plane(x, axis):
        return [lax.dynamic_index_in_dim(x, here ^ k, axis, keepdims=False) for k in range(plane)]

    def collect(sides):
        got = from_plane(
            [lax.dynamic_index_in_dim(sides[k // nl], l ^ (k % nl), 0, keepdims=False) for k in range(plane)]
        )
        return jnp.stack(got, axis=1)

    def to_parts(x):
        return jnp.stack(from_plane([x[k] for k in range(plane)]), axis=1)

    def scatter_y(sent, kept):
        total = sent
        for i, mine in enumerate(kept):
            total = turn(total, "y", ny).astype(F32) + mine.astype(F32)
            total = total.astype(LOW) if i < len(kept) - 1 else total
        return total

    def scatter_h(x):
        def block(i):
            return lax.dynamic_index_in_dim(x, (h - i) % nh, 0, keepdims=False)

        total = block(1 % nh)
        for i in range(2, nh + 1):
            total = turn(total.astype(LOW), "h", nh).astype(F32) + block(i % nh)
        return total

    def rows_of_y(x):
        out = [lax.dynamic_index_in_dim(x, (y - i) % ny, 0, keepdims=False) for i in range(1, ny + 1)]
        return out[0], out[1:]

    small = jnp.concatenate([gain_mix, gain_state, gain_ffn, lower_bound, starts.astype(F32)]).reshape(1, -1)
    small_mine = jnp.concatenate(from_plane([small] * plane))
    small_other = lax.ppermute(small_mine, "chip", [(i, i ^ 1) for i in range(nc)])
    plane_small = jnp.concatenate([pick(c == 0, small_mine, small_other), pick(c == 0, small_other, small_mine)])
    spread = lambda w: w.reshape(r, plane, nc, part)
    three = jnp.concatenate([spread(w_forget), spread(w_input), spread(w_query)], axis=3).transpose(2, 1, 0, 3)
    three = jnp.concatenate(from_plane(at_plane(to_cores(three), 1)))
    out_line = turns(w_output, "h", nh)
    out_first = turns(w_output, "y", ny)
    tokens_pair = jnp.concatenate([tokens, swap(tokens, "l")])
    vectors = jnp.stack(turns(plane_small[:, : 4 * r], "y", ny))
    vectors = jnp.concatenate(turns(vectors, "h", nh)).reshape(plan.devices, -1)
    (packed,) = call(partial(pack_kernel, plan, ffr), [shape((nc, plane, r, 2 * units), LOW)], w_gate, w_up)
    packed = to_cores(after(packed, out_line))
    plane_small, three, out_line, out_first, tokens_pair, packed, vectors, cotangent, w_down = fence(
        plane_small, three, out_line, out_first, tokens_pair, packed, vectors, cotangent, w_down
    )

    three_line = turns(three, "h", nh)
    three_first = turns(three, "y", ny)
    out_copies = out_first + [z for x in out_line[1:] for z in turns(after(x, three_first), "y", ny)]
    tokens_far = swap(tokens_pair, "x")
    gate_up = from_plane(at_plane(packed, 1))
    gate_up = [jnp.concatenate(gate_up[:nl]), jnp.concatenate(gate_up[nl:])]
    three_line, three_first, out_copies, tokens_pair, tokens_far, gate_up, cotangent, w_down = fence(
        three_line, three_first, out_copies, tokens_pair, tokens_far, gate_up, cotangent, w_down
    )

    three = three_first + [z for x in three_line[1:] for z in turns(x, "y", ny)]
    gu_first = jnp.stack(turns(gate_up[0], "h", nh))
    plane_tokens = over_plane([tokens_pair, tokens_far])
    plane_starts = (
        plane_small[:, 4 * r :].reshape(nc, nx, nl, rows).transpose(1, 2, 0, 3).reshape(nx, span)
    )
    starts_row = jnp.broadcast_to(plane_starts[:, None], (nx, 8, span)).astype(LOW)
    starts_wide = jnp.broadcast_to(plane_starts[:, :, None], (nx, span, HDIM)).astype(LOW)
    places = jnp.stack([
        plan.owner((y - j) % ny, here ^ k, (h - i) % nh, e)
        for i in range(nh) for j in range(ny) for e in range(nc) for k in range(plane)
    ])
    ordered = (jnp.arange(plan.devices)[:, None] == places[None, :]).astype(F32)
    vectors = jnp.dot(ordered, vectors, precision=lax.Precision.HIGHEST)
    vectors = vectors.reshape(plan.devices, 4, r).transpose(1, 0, 2).reshape(4, width)
    full_gain_mix, full_gain_state, full_gain_ffn = (vectors[i : i + 1] for i in range(3))
    lower = lax.dynamic_slice_in_dim(vectors[3], (here * nc + c) * part, part).reshape(heads, 1, HDIM)
    count = plan.devices
    total = nc * half
    project_flops = 2 * total * width * 3 * part
    normed_in, pre, w_three = call(
        partial(project_kernel, plan, names),
        [shape((total, width), LOW), shape((total, 3 * part)), shape((count, r, 3 * part), LOW)],
        where, plane_tokens, full_gain_mix, *three,
        specs=[SMEM, VMEM, VMEM] + [ANY] * copies,
        scratch=[pltpu.SemaphoreType.DMA((count,))],
        flops=project_flops,
    )
    cut = copies // 2
    pieces = [jnp.stack(out_copies[:cut]), jnp.stack(out_copies[cut:])]
    moved = [swap(z, axis) for z, axis in zip(pieces, ("l", "x"))]
    cotangent_pair = jnp.concatenate([cotangent, swap(after(cotangent, moved), "l")])
    gate_up, pre, pieces, moved, lower, starts_wide, starts_row, gu_first, cotangent_pair, w_down = fence(
        gate_up, pre, pieces, moved, lower, starts_wide, starts_row, gu_first, cotangent_pair, w_down
    )

    by_group = lambda x: x.reshape(nc, nx, nl, rows, -1)
    piece = lambda i: pl.BlockSpec((nc, 1, nl, rows, HDIM), lambda g, a, i=i: (0, g, 0, 0, i * heads + a))
    state_spec = pl.BlockSpec((1, 1, HDIM, HDIM), lambda g, a: (g, a, 0, 0))
    rows_spec = pl.BlockSpec((1, 1, span, HDIM), lambda g, a: (g, a, 0, 0))
    scores_spec = pl.BlockSpec((1, 1, span, span), lambda g, a: (g, a, 0, 0))
    head_spec = pl.BlockSpec((1, 1, HDIM), lambda g, a: (a, 0, 0))
    starts_spec = pl.BlockSpec((1, span, HDIM), lambda g, a: (g, 0, 0))
    starts_row_spec = pl.BlockSpec((1, 8, span), lambda g, a: (g, 0, 0))
    pre_args = (by_group(pre),) * 3
    pre_specs = [piece(0), piece(1), piece(2)]
    states = (nx, heads, HDIM, HDIM)
    by_row = (nx, heads, span, HDIM)
    grouped = (nc, nx, nl, rows, part)
    mix_flops = nx * heads * 2 * span * span * HDIM
    end_state, decay, local, query_reach, cumulative, scores = call(
        mix_kernel,
        [shape(states), shape(states), shape(by_row), shape(by_row, LOW), shape(by_row),
         shape((nx, heads, span, span), LOW)],
        where, *pre_args, lower, starts_wide, starts_row,
        grid=(nx, heads),
        specs=[SMEM] + pre_specs + [head_spec, starts_spec, starts_row_spec],
        out_specs=[state_spec, state_spec, rows_spec, rows_spec, rows_spec, scores_spec],
        flops=8 * mix_flops,
    )
    gu_first = turns(gu_first, "y", ny)
    gu_second = jnp.stack(turns(gate_up[1], "h", nh))
    pairs = [jnp.stack([a, z]) for a, z in zip(pieces, moved)]
    moved = [swap(z, axis) for z, axis in zip(pairs, ("x", "l"))]
    groups = jnp.stack([pairs[0], moved[0], pairs[1], moved[1]])
    out_names = [
        (t * 2 + distance, u, m, *names[t * cut + m], u * nl + distance if t else distance * nl + u)
        for t in range(2) for distance in range(2) for u in range(2) for m in range(cut)
    ]
    end_state, decay, local, query_reach, gu_first, groups, gu_second, cotangent_pair, w_down = fence(
        end_state, decay, local, query_reach, gu_first, groups, gu_second, cotangent_pair, w_down
    )

    def carry(block, step):
        incoming = jnp.zeros_like(block)
        for t in range(nh - 1):
            pairs = [(i, i + step) for i in range(nh) if 0 <= i + step < nh]
            sent = decay * incoming + block if t else block
            incoming = lax.ppermute(sent.astype(LOW), "h", pairs)
            incoming = incoming if t == nh - 2 else incoming.astype(F32)
        return incoming

    incoming = carry(end_state, 1)
    (mixed,) = call(
        mix_end_kernel, [shape(grouped, LOW)], local, query_reach, incoming,
        grid=(nx, heads), specs=[rows_spec, rows_spec, state_spec], out_specs=[piece(0)], flops=mix_flops // 4,
    )
    mixed = to_cores(mixed.reshape(nc, plane, rows, part))
    down_line = turns(after(w_down, incoming), "h", nh)
    mixed_in = from_plane(after([mixed[:, k] for k in range(plane)], down_line))
    gate_up = gu_first + turns(gu_second, "y", ny)
    cotangent_far = swap(cotangent_pair, "x")
    groups_other = lax.ppermute(groups, "chip", [(i, i ^ 1) for i in range(nc)])
    plane_cotangent = over_plane([cotangent_pair, cotangent_far])
    mixed_in, gate_up, groups, groups_other, plane_cotangent, down_line = fence(
        mixed_in, gate_up, groups, groups_other, plane_cotangent, down_line
    )

    parts_shape = (plane, nc, rows, part)
    mixed, normed_parts, residual, normed_ffn, w_out_full = call(
        partial(branch_kernel, plan, out_names, part),
        [shape((rows, width)), shape(parts_shape, LOW), shape((rows, width)), shape((rows, width), LOW),
         shape((count, r, width), LOW)],
        where, tokens, full_gain_state, full_gain_ffn, *mixed_in, groups, groups_other,
        specs=[SMEM] + [VMEM] * (3 + plane) + [ANY] * 2,
        scratch=[pltpu.SemaphoreType.DMA((count,))],
        flops=2 * rows * width * width,
    )
    ffn_pieces = from_plane([normed_ffn] * plane)
    down = jnp.zeros((ny, nh, ffr, width), LOW)
    for j, blocks in enumerate(turns(jnp.stack(down_line), "y", ny)):
        for i in range(nh):
            down = lax.dynamic_update_slice(down, blocks[i][None, None], ((y - j) % ny, (h - i) % nh, 0, 0))
    down = down.reshape(units, width)
    ffn_pieces, gate_up, down, normed_parts, plane_cotangent = fence(
        ffn_pieces, gate_up, down, normed_parts, plane_cotangent
    )

    plane_ffn = over_plane(ffn_pieces)
    gu_names = [(j, k) for k in (0, nl) for j in range(ny)]
    step = min(256, half)
    row_spec = lambda n: pl.BlockSpec((step, n), lambda t: (t, 0))
    hidden, grad_gu, part_out, part_ffn = call(
        partial(ffn_kernel, plan, gu_names),
        [shape((total, units), LOW), shape((total, 2 * units), LOW), shape((total, width), LOW),
         shape((total, width), LOW)],
        where, plane_ffn, plane_cotangent, down, *gate_up,
        grid=(total // step,),
        specs=[SMEM, row_spec(width), row_spec(width), VMEM] + [ANY] * len(gate_up),
        out_specs=[row_spec(units), row_spec(2 * units), row_spec(width), row_spec(width)],
        scratch=[pltpu.VMEM((count, r, 2 * units), LOW), pltpu.SemaphoreType.DMA((count,))],
        flops=2 * total * width * units * 7,
    )
    lcr = nl * nc * r

    def columns_grad(turns, dtype, sides, normed, grads):
        n = sum(g.shape[1] for g in grads)
        return call(
            partial(columns_grad_kernel, plan, turns, sides, len(grads)), [shape((nh, len(sides), lcr, n), dtype)],
            where, normed, *grads, specs=[SMEM] + [VMEM] * (1 + len(grads)),
            flops=2 * total * width * n * len(sides) // (ny * nx),
        )[0]

    def columns_kept(sides, *arrays):
        return [columns_grad(i % ny, F32 if i == ny else LOW, sides, *arrays) for i in range(2, ny + 1)]

    both_ffn = summed_core(part_ffn)
    far_sent = columns_grad(1, LOW, (1,), plane_ffn, [grad_gu])
    mix_parts = to_parts(after(normed_parts, plane_ffn))
    both_ffn, far_sent, plane_ffn, grad_gu, hidden, mix_parts, plane_cotangent, part_out = fence(
        both_ffn, far_sent, plane_ffn, grad_gu, hidden, mix_parts, plane_cotangent, part_out
    )

    grad_normed_ffn = summed_plane(both_ffn)
    near_sent = columns_grad(1, LOW, (0,), plane_ffn, [grad_gu])
    grad_gu_far = scatter_y(far_sent, columns_kept((1,), plane_ffn, [grad_gu]))
    (grad_down,) = call(
        rows_grad_kernel, [shape((units, width), LOW)], hidden, plane_cotangent, flops=2 * total * units * width,
    )
    both_out = summed_core(after(part_out, grad_down))
    grad_gu_far, grad_normed_ffn, near_sent, grad_down, plane_ffn, grad_gu, both_out = fence(
        grad_gu_far, grad_normed_ffn, near_sent, grad_down, plane_ffn, grad_gu, both_out
    )

    grad_gu_near = scatter_y(near_sent, columns_kept((0,), plane_ffn, [grad_gu]))
    grad_residual, branch, grad_parts = call(
        partial(branch_back_kernel, plan, part),
        [shape((rows, width)), shape((rows, width), LOW), shape(parts_shape, LOW)],
        where, grad_normed_ffn, cotangent, residual, mixed, full_gain_state, full_gain_ffn, w_out_full,
        specs=[SMEM] + [VMEM] * 7,
        scratch=[pltpu.VMEM((rows, width), LOW)],
        flops=2 * rows * width * width,
    )
    grads = to_parts(grad_parts)
    grad_gu_far = scatter_h(after(grad_gu_far, grads))
    output = (residual + summed_plane(after(both_out, grads))).astype(LOW)
    grads = by_group(to_cores(grads))
    (state_grad,) = call(
        mix_state_grad_kernel, [shape(states)], query_reach, grads,
        grid=(nx, heads), specs=[rows_spec, piece(0)], out_specs=[state_spec], flops=mix_flops // 4,
    )
    grad_gu_near, state_grad, grads, branch, grad_gu_far, output, grad_down = fence(
        grad_gu_near, state_grad, grads, branch, grad_gu_far, output, grad_down
    )

    next_grad = carry(state_grad, -1)
    grad_gu_near = scatter_h(after(grad_gu_near, next_grad))
    branch_pieces = from_plane([branch] * plane)
    grad_down = scatter_y(*rows_of_y(grad_down.reshape(ny, nh, ffr, width)))
    df, dv, dq, lower_grad = call(
        mix_back_kernel,
        [shape(grouped, LOW)] * 3 + [shape((nx, heads, 8, HDIM))],
        where, *pre_args, lower, starts_wide, starts_row, cumulative, scores, grads, incoming, next_grad, decay,
        grid=(nx, heads),
        specs=[SMEM] + pre_specs + [head_spec, starts_spec, starts_row_spec, rows_spec, scores_spec]
        + [piece(0), state_spec, state_spec, state_spec],
        out_specs=[piece(0)] * 3 + [pl.BlockSpec((1, 1, 8, HDIM), lambda g, a: (g, a, 0, 0))],
        flops=12 * mix_flops,
    )
    pre_grads = [g.reshape(total, part) for g in (df, dv, dq)]
    (part_in,) = call(
        inputs_grad_kernel, [shape((total, width), LOW)], *pre_grads, w_three, flops=project_flops
    )
    both_in = summed_core(part_in)
    three_sent = columns_grad(1, LOW, (0, 1), normed_in, after(pre_grads, grad_gu_near))
    both_in, three_sent, pre_grads, branch_pieces, grad_gu_near, grad_gu_far, grad_down = fence(
        both_in, three_sent, pre_grads, branch_pieces, grad_gu_near, grad_gu_far, grad_down
    )

    grad_normed_in = summed_plane(both_in)
    grad_three = scatter_y(three_sent, columns_kept((0, 1), normed_in, pre_grads))
    grad_down = scatter_h(grad_down)
    (grad_out,) = call(
        rows_grad_kernel, [shape((part, width), LOW)], to_cores(mix_parts).reshape(total, part), over_plane(branch_pieces),
        flops=2 * total * part * width,
    )
    grad_three, grad_normed_in, grad_gu_near, grad_out, grad_gu_far, grad_down = fence(
        grad_three, grad_normed_in, grad_gu_near, grad_out, grad_gu_far, grad_down
    )

    own_tokens = tokens.astype(F32)
    grad_tokens = grad_residual + norm_back(own_tokens, inverse_rms(own_tokens), grad_normed_in * full_gain_mix)
    grad_three = scatter_h(grad_three).astype(LOW).reshape(nx, nl, nc, r, 3 * part)
    grad_output = scatter_y(*rows_of_y(grad_out.reshape(ny, nh, r, width)))
    gu_blocks = collect([z.astype(LOW).reshape(nl, nc, r, 2 * units) for z in (grad_gu_near, grad_gu_far)])
    lower_grad = jnp.sum(lower_grad[:, :, 0], axis=0).reshape(1, part)
    lower_grad = sum(turns(after(lower_grad, grad_output), "y", ny))
    grad_three, grad_output, gu_blocks, lower_grad = fence(
        grad_three, grad_output, gu_blocks, lower_grad
    )

    three_blocks = collect([grad_three[t] for t in range(nx)])
    grad_output = scatter_h(grad_output)
    lower_grad = sum(turns(after(lower_grad, grad_output), "h", nh))
    owners = []
    for j in range(ny):
        for p in range(nx):
            for i in range(nh):
                for o in range(nl):
                    for e in range(nc):
                        owners.append(((p * nl + o) * nc + e) * copies + j * nh + i)
    pairs = list(enumerate(owners))
    along = shape((r, HDIM))
    grad_w_gate, grad_w_up, along_ffn = call(
        partial(unpack_kernel, plan, ffr), [shape(w_gate.shape), shape(w_up.shape), along],
        where, to_cores(gu_blocks), w_gate, w_up, specs=[SMEM] + [VMEM] * 3,
        scratch=[pltpu.VMEM((nc, plane, r, 2 * units), LOW)],
    )
    grad_w_forget, grad_w_input, grad_w_query, along_mix = call(
        partial(unpack_part_kernel, plan, part), [shape(w_query.shape)] * 3 + [along],
        where, to_cores(three_blocks), w_forget, w_input, w_query, specs=[SMEM] + [VMEM] * 4,
    )
    grad_output = lax.ppermute(grad_output.astype(LOW), AXES, pairs).astype(F32)
    lower_grad = lax.dynamic_index_in_dim(lower_grad.reshape(copies, r), y * nh + h, 0, keepdims=False)
    lower_grad = lax.ppermute(lower_grad, AXES, pairs)
    grad_gain_mix = along_mix[:, 0] / gain_mix
    grad_gain_ffn = along_ffn[:, 0] / gain_ffn
    grad_gain_state = jnp.sum(w_output.astype(F32) * grad_output, axis=1) / gain_state
    return (
        output, grad_tokens, grad_w_query, grad_w_forget, grad_w_input, grad_output, grad_gain_mix, lower_grad,
        grad_gain_state, grad_w_gate, grad_w_up, grad_down, grad_gain_ffn,
    )


def solution(mesh):
    nb, ns, nc = (mesh.shape[a] for a in ("batch", "seq", "chip"))
    sizes = (nb // 2, 2, ns // 2, 2, nc)
    fine = jax.sharding.Mesh(mesh.devices.reshape(sizes), AXES)
    flat, matrix = P(AXES), P(AXES, None)
    return jax.shard_map(
        partial(body, Plan(sizes)),
        mesh=fine,
        in_specs=(
            matrix, flat, matrix, matrix, matrix, matrix, flat, flat, flat, matrix, matrix, matrix, flat, matrix,
        ),
        out_specs=(
            matrix, matrix, matrix, matrix, matrix, matrix, flat, flat, flat, matrix, matrix, matrix, flat,
        ),
        check_vma=False,
    )
```

```python
import math
from functools import partial

import jax
import jax.numpy as jnp
from jax import lax
from jax.experimental import pallas as pl
from jax.experimental.pallas import tpu as pltpu
from jax.sharding import PartitionSpec as P

HDIM = 128
EPSILON = 1e-06
RESET_LOG = -30.0
F32 = jnp.float32
LOW = jnp.bfloat16
AXES = ("y", "x", "h", "l", "chip")
LIMIT = 56 * 2**20
VMEM = pl.BlockSpec(memory_space=pltpu.VMEM)
SMEM = pl.BlockSpec(memory_space=pltpu.SMEM)
ANY = pl.BlockSpec(memory_space=pl.ANY)


def dot(left, right):
    return jnp.dot(left, right, preferred_element_type=F32)


def dot_tn(left, right):
    return lax.dot_general(left, right, (((0,), (0,)), ((), ())), preferred_element_type=F32)


def dot_nt(left, right):
    return lax.dot_general(left, right, (((1,), (1,)), ((), ())), preferred_element_type=F32)


def inverse_rms(values):
    return lax.rsqrt(jnp.mean(values * values, axis=-1, keepdims=True) + EPSILON)


def norm_back(values, rms, scaled):
    inner = jnp.mean(scaled * values, axis=-1, keepdims=True)
    return rms * scaled - values * (rms * rms * rms * inner)


def sigmoid(a):
    return 1.0 / (1.0 + jnp.exp(-a))


def pick(flag, first, second):
    return jnp.where(flag, first, second)


def after(x, *deps):
    return lax.optimization_barrier((x, deps))[0]


def shape(dims, dtype=F32):
    return jax.ShapeDtypeStruct(tuple(dims), dtype)


def call(kernel, outs, *args, specs=None, out_specs=None, grid=(), scratch=(), flops=0):
    outs = tuple(outs)
    specs = [VMEM] * len(args) if specs is None else specs
    out_specs = tuple([VMEM] * len(outs)) if out_specs is None else tuple(out_specs)
    moved = sum(math.prod(a.shape) * a.dtype.itemsize for a in (*args, *outs))
    return pl.pallas_call(
        kernel,
        out_shape=outs,
        grid=grid,
        in_specs=specs,
        out_specs=out_specs,
        scratch_shapes=list(scratch),
        compiler_params=pltpu.CompilerParams(vmem_limit_bytes=LIMIT),
        cost_estimate=pl.CostEstimate(flops=int(flops) // 8, bytes_accessed=int(moved) // 8, transcendentals=0),
    )(*args)


class Plan:
    def __init__(self, sizes):
        self.ny, self.nx, self.nh, self.nl, self.nc = sizes
        self.plane = self.nx * self.nl
        self.copies = self.ny * self.nh
        self.devices = self.copies * self.plane * self.nc

    def owner(self, y, p, h, c):
        return (((y * self.nx + p // self.nl) * self.nh + h) * self.nl + p % self.nl) * self.nc + c


def fetch(plan, where, blocks, target, sems, start=True):
    y, h, here = (where[i] for i in range(3))
    moves = []
    for t, (source, i, j, k, e) in enumerate(blocks):
        yy = lax.rem(y + (plan.ny - j), plan.ny)
        hh = lax.rem(h + (plan.nh - i), plan.nh)
        place = plan.owner(yy, here ^ k, hh, e)
        move = pltpu.make_async_copy(source, target.at[place], sems.at[t])
        if start:
            move.start()
        moves.append(move)
    return moves


def pack_kernel(plan, ffr, gate, up, out):
    units = plan.copies * ffr
    for e in range(plan.nc):
        for p in range(plan.plane):
            for w, base in ((gate, 0), (up, units)):
                for m in range(plan.copies):
                    at = plan.owner(m // plan.nh, p, m % plan.nh, e) * ffr
                    to = base + m * ffr
                    out[e, p, :, to : to + ffr] = w[:, at : at + ffr]


def unpack_kernel(plan, ffr, where, blocks, gate, up, grad_gate, grad_up, along, ordered):
    here = where[2]
    units = plan.copies * ffr
    for k in range(plan.plane):
        for e in range(plan.nc):
            ordered[e, here ^ k] = blocks[e, k]
    for e in range(plan.nc):
        for p in range(plan.plane):
            block = ordered[e, p].astype(F32)
            for g, base in ((grad_gate, 0), (grad_up, units)):
                for m in range(plan.copies):
                    at = plan.owner(m // plan.nh, p, m % plan.nh, e) * ffr
                    to = base + m * ffr
                    g[:, at : at + ffr] = block[:, to : to + ffr]
    total = jnp.sum(gate[...].astype(F32) * grad_gate[...], axis=1, keepdims=True)
    total = total + jnp.sum(up[...].astype(F32) * grad_up[...], axis=1, keepdims=True)
    along[...] = jnp.broadcast_to(total, along.shape)


def unpack_part_kernel(plan, part, where, blocks, w0, w1, w2, g0, g1, g2, along):
    here = where[2]
    for k in range(plan.plane):
        for e in range(plan.nc):
            at = pl.multiple_of(((here ^ k) * plan.nc + e) * part, part)
            for i, g in enumerate((g0, g1, g2)):
                g[:, pl.ds(at, part)] = blocks[e, k, :, i * part : (i + 1) * part].astype(F32)
    total = 0.0
    for w, g in ((w0, g0), (w1, g1), (w2, g2)):
        total = total + jnp.sum(w[...].astype(F32) * g[...], axis=1, keepdims=True)
    along[...] = jnp.broadcast_to(total, along.shape)


def normalize(x, gain, out, step):
    @pl.loop(0, x.shape[0] // step)
    def _(t):
        at = pl.ds(pl.multiple_of(t * step, step), step)
        values = x[at, :].astype(F32)
        out[at, :] = (values * inverse_rms(values) * gain[...]).astype(LOW)


def project_kernel(plan, names, where, x, gain, *rest):
    blocks, (normed, pre, weight, sems) = rest[: len(names)], rest[len(names) :]
    moves = fetch(
        plan, where,
        [(ref.at[k * plan.nc + e], i, j, k, e) for ref, (i, j) in zip(blocks, names)
         for k in range(plan.plane) for e in range(plan.nc)],
        weight, sems,
    )
    normalize(x, gain, normed, 64)
    for move in moves:
        move.wait()
    pre[...] = dot(normed[...], weight[...].reshape(-1, weight.shape[-1]))


def ffn_kernel(plan, names, where, normed, cotangent, down, *rest):
    blocks, (hidden, grad_gu, part_out, part_grad, weight, sems) = rest[: len(names)], rest[len(names) :]
    first = pl.program_id(0) == 0

    def moves(start):
        return fetch(
            plan, where,
            [(ref.at[i, k * plan.nc + e], i, j, base + k, e) for ref, (j, base) in zip(blocks, names)
             for i in range(plan.nh) for k in range(ref.shape[1] // plan.nc) for e in range(plan.nc)],
            weight, sems, start,
        )

    @pl.when(first)
    def _():
        moves(True)

    units = down.shape[0]
    upstream = dot_nt(cotangent[...], down[...])

    @pl.when(first)
    def _():
        for move in moves(False):
            move.wait()

    full = weight[...].reshape(-1, weight.shape[-1])
    both = dot(normed[...], full)
    gate, up = both[:, :units], both[:, units:]
    sig = sigmoid(gate)
    silu = gate * sig
    hid = (silu * up).astype(LOW)
    hidden[...] = hid
    grad_gu[:, :units] = (upstream * up * sig * (1.0 + gate * (1.0 - sig))).astype(LOW)
    grad_gu[:, units:] = (upstream * silu).astype(LOW)
    part_grad[...] = dot_nt(grad_gu[...], full).astype(part_grad.dtype)
    part_out[...] = dot(hid, down[...]).astype(part_out.dtype)


def columns_grad_kernel(plan, turn, sides, count, where, normed, *rest):
    grads, out = rest[:count], rest[count]
    y = lax.rem(where[0] + (plan.ny - turn), plan.ny)
    step = out.shape[0] * out.shape[2]
    for t, side in enumerate(sides):
        at = pl.multiple_of((y * plan.nx + (where[5] ^ side)) * step, step)
        base = 0
        for a in grads:
            n = a.shape[1]
            value = dot_tn(normed[:, pl.ds(at, step)], a[...])
            for i in range(plan.nh):
                out[i, t, :, base : base + n] = value[i * out.shape[2] : (i + 1) * out.shape[2]].astype(out.dtype)
            base += n


def rows_grad_kernel(left, right, out):
    n = 512
    for t in range(out.shape[1] // n):
        at = slice(t * n, (t + 1) * n)
        out[:, at] = dot_tn(left[...], right[:, at]).astype(out.dtype)


def interleaved(x):
    return jnp.concatenate([x[e, 0, i] for i in range(x.shape[2]) for e in range(x.shape[0])], axis=0)


def separated(x, out):
    nc, _, nl, rows, _ = out.shape
    for i in range(nl):
        for e in range(nc):
            at = (i * nc + e) * rows
            out[e, 0, i] = x[at : at + rows].astype(out.dtype)


def thirds(x):
    first = x.astype(LOW)
    rest = x - first.astype(F32)
    second = rest.astype(LOW)
    return first, second, (rest - second.astype(F32)).astype(LOW)


def causal_of(where, span, rows):
    flip = where[4] * rows
    t = lax.broadcasted_iota(jnp.int32, (span, span), 0) ^ flip
    s = lax.broadcasted_iota(jnp.int32, (span, span), 1) ^ flip
    return (t >= s).astype(F32)


def gate_terms(forget_pre, lower, is_start):
    sig = sigmoid(forget_pre)
    gate = lower + (1.0 - lower) * sig
    return sig, gate, 1.0 - gate, jnp.where(is_start, 0.0, jnp.log(gate))


def decay_terms(causal, starts, starts_row, cumulative, total):
    low = causal.astype(LOW)
    count = dot(low, starts)
    count_row = dot_nt(starts_row, low)[:1]
    ends = jnp.sum(starts.astype(F32), axis=0, keepdims=True)
    reach = jnp.exp(RESET_LOG * count)
    left = jnp.exp(RESET_LOG * (ends - count))
    between = causal * jnp.exp(RESET_LOG * jnp.maximum(count[:, :1] - count_row, 0.0))
    return reach, between, jnp.exp(cumulative), jnp.exp(-cumulative), jnp.exp(total - cumulative) * left, ends


def mix_kernel(
    where, f, v, q, lower, starts, starts_row,
    end_state, decay, local, query_reach, cumulative_out, scores_out,
):
    rows = f.shape[3]
    forget_pre, value, query_pre = interleaved(f), interleaved(v), interleaved(q)
    span = forget_pre.shape[0]
    is_start = starts[0].astype(F32) == 1.0
    _, _, key, log_decay = gate_terms(forget_pre, lower[0], is_start)
    causal = causal_of(where, span, rows)
    low = causal.astype(LOW)
    parts = thirds(log_decay)
    cumulative = dot(low, parts[0]) + dot(low, parts[1]) + dot(low, parts[2])
    total = jnp.sum(log_decay, axis=0, keepdims=True)
    reach, between, grow, shrink, suffix, ends = decay_terms(causal, starts[0], starts_row[0], cumulative, total)
    query = query_pre * sigmoid(query_pre) * grow
    value_low = value.astype(LOW)
    end_state[0, 0] = dot_tn((key * suffix).astype(LOW), value_low)
    ones = jnp.ones((span, HDIM), LOW)
    total_column = dot_tn(parts[0], ones) + dot_tn(parts[1], ones) + dot_tn(parts[2], ones)
    decay[0, 0] = jnp.exp(total_column + RESET_LOG * ends)
    scores = (dot_nt(query.astype(LOW), (key * shrink).astype(LOW)) * between).astype(LOW)
    local[0, 0] = dot(scores, value_low)
    query_reach[0, 0] = (query * reach).astype(LOW)
    cumulative_out[0, 0] = cumulative
    scores_out[0, 0] = scores


def mix_end_kernel(local, query_reach, incoming, out):
    separated(local[0, 0] + dot(query_reach[0, 0], incoming[0, 0]), out)


def mix_state_grad_kernel(query_reach, grads, out):
    out[0, 0] = dot_tn(query_reach[0, 0], interleaved(grads))


def mix_back_kernel(
    where, f, v, q, lower, starts, starts_row, cumulative_in, scores_in, grads, incoming, next_grad, decay,
    df, dv, dq, lower_grad,
):
    rows = f.shape[3]
    forget_pre, value, query_pre, upstream = interleaved(f), interleaved(v), interleaved(q), interleaved(grads)
    span = forget_pre.shape[0]
    is_start = starts[0].astype(F32) == 1.0
    low_bound = lower[0]
    forget_sig, gate, key, log_decay = gate_terms(forget_pre, low_bound, is_start)
    causal = causal_of(where, span, rows)
    low = causal.astype(LOW)
    cumulative = cumulative_in[0, 0]
    total = jnp.sum(log_decay, axis=0, keepdims=True)
    reach, between, grow, shrink, suffix, _ = decay_terms(causal, starts[0], starts_row[0], cumulative, total)
    query_sig = sigmoid(query_pre)
    query_ext = (query_pre * query_sig * grow).astype(LOW)
    key_shrink = (key * shrink).astype(LOW)
    key_suffix = (key * suffix).astype(LOW)
    value_low = value.astype(LOW)
    state, after_state = incoming[0, 0], next_grad[0, 0]
    grad_scores = (dot_nt(upstream, value_low) * between).astype(LOW)
    grad_ext = dot(grad_scores, key_shrink) + reach * dot_nt(upstream, state)
    grad_shrink = dot_tn(grad_scores, query_ext)
    grad_suffix = dot_nt(value_low, after_state)
    grad_value = dot_tn(scores_in[0, 0], upstream) + dot(key_suffix, after_state)
    suffix_term = key_suffix.astype(F32) * grad_suffix
    terms = query_ext.astype(F32) * grad_ext - key_shrink.astype(F32) * grad_shrink - suffix_term
    ones = jnp.ones((8, HDIM), LOW)
    state_term = thirds(decay[0, 0] * state.astype(F32) * after_state.astype(F32))
    state_row = (dot_nt(ones, state_term[0]) + dot_nt(ones, state_term[1]) + dot_nt(ones, state_term[2]))[:1]
    grad_total = jnp.sum(suffix_term, axis=0, keepdims=True) + state_row
    parts = thirds(terms)
    grad_log = dot_tn(low, parts[0]) + dot_tn(low, parts[1]) + dot_tn(low, parts[2]) + grad_total
    grad_key = grad_shrink * shrink + grad_suffix * suffix
    grad_forget = jnp.where(is_start, 0.0, grad_log / gate) - grad_key
    lower_grad[0, 0] = jnp.broadcast_to(
        jnp.sum(grad_forget * (1.0 - forget_sig), axis=0, keepdims=True), lower_grad.shape[2:]
    )
    separated(grad_forget * (1.0 - low_bound) * forget_sig * (1.0 - forget_sig), df)
    separated(grad_value, dv)
    separated(grad_ext * grow * query_sig * (1.0 + query_pre * (1.0 - query_sig)), dq)


def branch_kernel(plan, names, part, where, tokens, gain_state, gain_ffn, *rest):
    mixed_in, rest = rest[: plan.plane], rest[plan.plane :]
    own, other, mixed, normed_parts, residual, normed_ffn, weight, sems = rest
    here = where[2]
    moves = fetch(
        plan, where,
        [(ref.at[t, u, m], i, j, k, e) for ref, e in ((own, where[3]), (other, where[3] ^ 1)) for t, u, m, i, j, k in names],
        weight, sems,
    )
    for k in range(plan.plane):
        for e in range(plan.nc):
            at = pl.multiple_of(((here ^ k) * plan.nc + e) * part, part)
            mixed[:, pl.ds(at, part)] = mixed_in[k][e].astype(F32)
    values = mixed[...]
    normed = (values * inverse_rms(values) * gain_state[...]).astype(LOW)
    normed_ffn[...] = normed
    for k in range(plan.plane):
        for e in range(plan.nc):
            at = pl.multiple_of(((here ^ k) * plan.nc + e) * part, part)
            normed_parts[k, e] = normed_ffn[:, pl.ds(at, part)]
    for move in moves:
        move.wait()
    total = tokens[...].astype(F32) + dot(normed, weight[...].reshape(-1, weight.shape[-1]))
    residual[...] = total
    normed_ffn[...] = (total * inverse_rms(total) * gain_ffn[...]).astype(LOW)


def branch_back_kernel(
    plan, part, where, upstream, cotangent, residual, mixed, gain_state, gain_ffn, weight,
    grad_residual, branch, grad_parts, scratch,
):
    here = where[2]
    values = residual[...]
    grad = cotangent[...].astype(F32) + norm_back(values, inverse_rms(values), upstream[...] * gain_ffn[...])
    grad_residual[...] = grad
    low = grad.astype(LOW)
    branch[...] = low
    values = mixed[...]
    scaled = dot_nt(low, weight[...].reshape(-1, weight.shape[-1])) * gain_state[...]
    scratch[...] = norm_back(values, inverse_rms(values), scaled).astype(LOW)
    for k in range(plan.plane):
        for e in range(plan.nc):
            at = pl.multiple_of(((here ^ k) * plan.nc + e) * part, part)
            grad_parts[k, e] = scratch[:, pl.ds(at, part)]


def inputs_grad_kernel(df, dv, dq, weight, out):
    part = df.shape[1]
    full = weight[...].reshape(-1, weight.shape[-1])
    out[...] = (
        dot_nt(df[...], full[:, :part]) + dot_nt(dv[...], full[:, part : 2 * part])
        + dot_nt(dq[...], full[:, 2 * part :])
    ).astype(out.dtype)


def body(
    plan, tokens, starts, w_query, w_forget, w_input, w_output, gain_mix, lower_bound, gain_state,
    w_gate, w_up, w_down, gain_ffn, cotangent,
):
    ny, nx, nh, nl, nc, plane, copies = (
        plan.ny, plan.nx, plan.nh, plan.nl, plan.nc, plan.plane, plan.copies
    )
    y, x_, h, l, c = (lax.axis_index(a) for a in AXES)
    here = x_ * nl + l
    where = jnp.stack([y, h, here, c, l * nc, x_]).astype(jnp.int32)
    rows, width = tokens.shape
    r = w_query.shape[0]
    part = width // (plane * nc)
    ffr = w_down.shape[0]
    units = copies * ffr
    heads = part // HDIM
    span = nl * nc * rows
    half = plane * rows
    names = [(i, j) for i in range(nh) for j in range(ny)]

    def fence(*values):
        return lax.optimization_barrier(values)

    def from_plane(blocks):
        return [blocks[0]] + [
            lax.ppermute(blocks[k], ("x", "l"), [(i, i ^ k) for i in range(plane)]) for k in range(1, plane)
        ]

    def swap(x, axis):
        return lax.ppermute(x, axis, [(0, 1), (1, 0)])

    def to_cores(x):
        return lax.all_to_all(x, "chip", 0, 0, tiled=True)

    def turn(x, axis, n):
        return lax.ppermute(x, axis, [(i, (i + 1) % n) for i in range(n)])

    def turns(x, axis, n):
        out = [x]
        for _ in range(1, n):
            out.append(turn(out[-1], axis, n))
        return out

    def over_plane(pieces):
        mine = jnp.concatenate(pieces)
        return to_cores(jnp.stack([mine, mine])).reshape(nc * mine.shape[0], -1)

    def summed_core(x):
        x = to_cores(x.reshape(nc, plane, rows, -1))
        sums = [x[0, k].astype(F32) + x[1, k].astype(F32) for k in range(plane)]
        return [sums[0]] + [z.astype(LOW) for z in sums[1:]]

    def summed_plane(sums):
        got = from_plane(sums)
        return sum((z.astype(F32) for z in got[1:]), got[0])

    def at_plane(x, axis):
        return [lax.dynamic_index_in_dim(x, here ^ k, axis, keepdims=False) for k in range(plane)]

    def collect(sides):
        got = from_plane(
            [lax.dynamic_index_in_dim(sides[k // nl], l ^ (k % nl), 0, keepdims=False) for k in range(plane)]
        )
        return jnp.stack(got, axis=1)

    def to_parts(x):
        return jnp.stack(from_plane([x[k] for k in range(plane)]), axis=1)

    def scatter_y(sent, kept):
        total = sent
        for i, mine in enumerate(kept):
            total = turn(total, "y", ny).astype(F32) + mine.astype(F32)
            total = total.astype(LOW) if i < len(kept) - 1 else total
        return total

    def scatter_h(x):
        def block(i):
            return lax.dynamic_index_in_dim(x, (h - i) % nh, 0, keepdims=False)

        total = block(1 % nh)
        for i in range(2, nh + 1):
            total = turn(total.astype(LOW), "h", nh).astype(F32) + block(i % nh)
        return total

    def rows_of_y(x):
        out = [lax.dynamic_index_in_dim(x, (y - i) % ny, 0, keepdims=False) for i in range(1, ny + 1)]
        return out[0], out[1:]

    spread = lambda w: w.reshape(r, plane, nc, part)
    three = jnp.concatenate([spread(w_forget), spread(w_input), spread(w_query)], axis=3).transpose(2, 1, 0, 3)
    three = to_cores(three)
    three = jnp.concatenate(from_plane(at_plane(three, 1)))
    small = jnp.concatenate([gain_mix, gain_state, gain_ffn, lower_bound, starts.astype(F32)]).reshape(1, -1)
    small_mine = jnp.concatenate(from_plane([after(small, three)] * plane))
    small_other = lax.ppermute(small_mine, "chip", [(i, i ^ 1) for i in range(nc)])
    plane_small = jnp.concatenate([pick(c == 0, small_mine, small_other), pick(c == 0, small_other, small_mine)])
    out_first = turns(w_output, "y", ny)
    tokens_pair = jnp.concatenate([tokens, swap(tokens, "l")])
    vectors = jnp.stack(turns(plane_small[:, : 4 * r], "y", ny))
    vectors = jnp.concatenate(turns(vectors, "h", nh)).reshape(plan.devices, -1)
    (packed,) = call(partial(pack_kernel, plan, ffr), [shape((nc, plane, r, 2 * units), LOW)], w_gate, w_up)
    packed = to_cores(packed)
    plane_small, three, w_output, out_first, tokens_pair, packed, vectors, cotangent, w_down = fence(
        plane_small, three, w_output, out_first, tokens_pair, packed, vectors, cotangent, w_down
    )

    three_line = turns(three, "h", nh)
    three_first = turns(three, "y", ny)
    out_line = turns(after(w_output, three_line), "h", nh)
    tokens_far = swap(tokens_pair, "x")
    gate_up = from_plane(at_plane(packed, 1))
    gate_up = [jnp.concatenate(gate_up[:nl]), jnp.concatenate(gate_up[nl:])]
    three_line, three_first, out_line, tokens_pair, tokens_far, gate_up, cotangent, w_down = fence(
        three_line, three_first, out_line, tokens_pair, tokens_far, gate_up, cotangent, w_down
    )

    three = three_first + [z for x in three_line[1:] for z in turns(x, "y", ny)]
    out_copies = out_first + [z for x in out_line[1:] for z in turns(x, "y", ny)]
    gu_line = turns(gate_up[0], "h", nh)
    plane_tokens = over_plane([tokens_pair, tokens_far])
    plane_starts = (
        plane_small[:, 4 * r :].reshape(nc, nx, nl, rows).transpose(1, 2, 0, 3).reshape(nx, span)
    )
    starts_row = jnp.broadcast_to(plane_starts[:, None], (nx, 8, span)).astype(LOW)
    starts_wide = jnp.broadcast_to(plane_starts[:, :, None], (nx, span, HDIM)).astype(LOW)
    places = jnp.stack([
        plan.owner((y - j) % ny, here ^ k, (h - i) % nh, e)
        for i in range(nh) for j in range(ny) for e in range(nc) for k in range(plane)
    ])
    ordered = (jnp.arange(plan.devices)[:, None] == places[None, :]).astype(F32)
    vectors = jnp.dot(ordered, vectors, precision=lax.Precision.HIGHEST)
    vectors = vectors.reshape(plan.devices, 4, r).transpose(1, 0, 2).reshape(4, width)
    full_gain_mix, full_gain_state, full_gain_ffn = (vectors[i : i + 1] for i in range(3))
    lower = lax.dynamic_slice_in_dim(vectors[3], (here * nc + c) * part, part).reshape(heads, 1, HDIM)
    count = plan.devices
    total = nc * half
    project_flops = 2 * total * width * 3 * part
    normed_in, pre, w_three = call(
        partial(project_kernel, plan, names),
        [shape((total, width), LOW), shape((total, 3 * part)), shape((count, r, 3 * part), LOW)],
        where, plane_tokens, full_gain_mix, *three,
        specs=[SMEM, VMEM, VMEM] + [ANY] * copies,
        scratch=[pltpu.SemaphoreType.DMA((count,))],
        flops=project_flops,
    )
    gu_first = jnp.stack(after(gu_line, pre))
    cut = copies // 2
    pieces = [jnp.stack(out_copies[:cut]), jnp.stack(out_copies[cut:])]
    moved = [swap(z, axis) for z, axis in zip(pieces, ("l", "x"))]
    cotangent_pair = jnp.concatenate([cotangent, swap(after(cotangent, moved), "l")])
    gate_up, pre, pieces, moved, lower, starts_wide, starts_row, gu_first, cotangent_pair, w_down = fence(
        gate_up, pre, pieces, moved, lower, starts_wide, starts_row, gu_first, cotangent_pair, w_down
    )

    by_group = lambda x: x.reshape(nc, nx, nl, rows, -1)
    piece = lambda i: pl.BlockSpec((nc, 1, nl, rows, HDIM), lambda g, a, i=i: (0, g, 0, 0, i * heads + a))
    state_spec = pl.BlockSpec((1, 1, HDIM, HDIM), lambda g, a: (g, a, 0, 0))
    rows_spec = pl.BlockSpec((1, 1, span, HDIM), lambda g, a: (g, a, 0, 0))
    scores_spec = pl.BlockSpec((1, 1, span, span), lambda g, a: (g, a, 0, 0))
    head_spec = pl.BlockSpec((1, 1, HDIM), lambda g, a: (a, 0, 0))
    starts_spec = pl.BlockSpec((1, span, HDIM), lambda g, a: (g, 0, 0))
    starts_row_spec = pl.BlockSpec((1, 8, span), lambda g, a: (g, 0, 0))
    pre_args = (by_group(pre),) * 3
    pre_specs = [piece(0), piece(1), piece(2)]
    states = (nx, heads, HDIM, HDIM)
    by_row = (nx, heads, span, HDIM)
    grouped = (nc, nx, nl, rows, part)
    mix_flops = nx * heads * 2 * span * span * HDIM
    end_state, decay, local, query_reach, cumulative, scores = call(
        mix_kernel,
        [shape(states), shape(states), shape(by_row), shape(by_row, LOW), shape(by_row),
         shape((nx, heads, span, span), LOW)],
        where, *pre_args, lower, starts_wide, starts_row,
        grid=(nx, heads),
        specs=[SMEM] + pre_specs + [head_spec, starts_spec, starts_row_spec],
        out_specs=[state_spec, state_spec, rows_spec, rows_spec, rows_spec, scores_spec],
        flops=8 * mix_flops,
    )
    gu_first = turns(gu_first, "y", ny)
    gu_second = jnp.stack(turns(gate_up[1], "h", nh))
    pairs = [jnp.stack([a, z]) for a, z in zip(pieces, moved)]
    moved = [swap(z, axis) for z, axis in zip(pairs, ("x", "l"))]
    groups = jnp.stack([pairs[0], moved[0], pairs[1], moved[1]])
    out_names = [
        (t * 2 + distance, u, m, *names[t * cut + m], u * nl + distance if t else distance * nl + u)
        for t in range(2) for distance in range(2) for u in range(2) for m in range(cut)
    ]
    end_state, decay, local, query_reach, gu_first, groups, gu_second, cotangent_pair, w_down = fence(
        end_state, decay, local, query_reach, gu_first, groups, gu_second, cotangent_pair, w_down
    )

    def carry(block, step):
        incoming = jnp.zeros_like(block)
        for t in range(nh - 1):
            pairs = [(i, i + step) for i in range(nh) if 0 <= i + step < nh]
            sent = decay * incoming + block if t else block
            incoming = lax.ppermute(sent.astype(LOW), "h", pairs)
            incoming = incoming if t == nh - 2 else incoming.astype(F32)
        return incoming

    incoming = carry(end_state, 1)
    (mixed,) = call(
        mix_end_kernel, [shape(grouped, LOW)], local, query_reach, incoming,
        grid=(nx, heads), specs=[rows_spec, rows_spec, state_spec], out_specs=[piece(0)], flops=mix_flops // 4,
    )
    mixed = to_cores(mixed.reshape(nc, plane, rows, part))
    down_line = turns(after(w_down, incoming), "h", nh)
    mixed_in = from_plane(after([mixed[:, k] for k in range(plane)], down_line))
    gate_up = gu_first + turns(gu_second, "y", ny)
    cotangent_far = swap(cotangent_pair, "x")
    groups_other = lax.ppermute(groups, "chip", [(i, i ^ 1) for i in range(nc)])
    plane_cotangent = over_plane([cotangent_pair, cotangent_far])
    mixed_in, gate_up, groups, groups_other, plane_cotangent, down_line = fence(
        mixed_in, gate_up, groups, groups_other, plane_cotangent, down_line
    )

    parts_shape = (plane, nc, rows, part)
    mixed, normed_parts, residual, normed_ffn, w_out_full = call(
        partial(branch_kernel, plan, out_names, part),
        [shape((rows, width)), shape(parts_shape, LOW), shape((rows, width)), shape((rows, width), LOW),
         shape((count, r, width), LOW)],
        where, tokens, full_gain_state, full_gain_ffn, *mixed_in, groups, groups_other,
        specs=[SMEM] + [VMEM] * (3 + plane) + [ANY] * 2,
        scratch=[pltpu.SemaphoreType.DMA((count,))],
        flops=2 * rows * width * width,
    )
    ffn_pieces = from_plane([normed_ffn] * plane)
    down = jnp.zeros((ny, nh, ffr, width), LOW)
    for j, blocks in enumerate(turns(jnp.stack(down_line), "y", ny)):
        for i in range(nh):
            down = lax.dynamic_update_slice(down, blocks[i][None, None], ((y - j) % ny, (h - i) % nh, 0, 0))
    down = down.reshape(units, width)
    ffn_pieces, gate_up, down, normed_parts, plane_cotangent = fence(
        ffn_pieces, gate_up, down, normed_parts, plane_cotangent
    )

    plane_ffn = over_plane(ffn_pieces)
    gu_names = [(j, k) for k in (0, nl) for j in range(ny)]
    step = half
    row_spec = lambda n: pl.BlockSpec((step, n), lambda t: (t, 0))
    hidden, grad_gu, part_out, part_ffn = call(
        partial(ffn_kernel, plan, gu_names),
        [shape((total, units), LOW), shape((total, 2 * units), LOW), shape((total, width), LOW),
         shape((total, width), LOW)],
        where, plane_ffn, plane_cotangent, down, *gate_up,
        grid=(total // step,),
        specs=[SMEM, row_spec(width), row_spec(width), VMEM] + [ANY] * len(gate_up),
        out_specs=[row_spec(units), row_spec(2 * units), row_spec(width), row_spec(width)],
        scratch=[pltpu.VMEM((count, r, 2 * units), LOW), pltpu.SemaphoreType.DMA((count,))],
        flops=2 * total * width * units * 7,
    )
    lcr = nl * nc * r

    def columns_grad(turns, dtype, sides, normed, grads):
        n = sum(g.shape[1] for g in grads)
        return call(
            partial(columns_grad_kernel, plan, turns, sides, len(grads)), [shape((nh, len(sides), lcr, n), dtype)],
            where, normed, *grads, specs=[SMEM] + [VMEM] * (1 + len(grads)),
            flops=2 * total * width * n * len(sides) // (ny * nx),
        )[0]

    def columns_kept(sides, *arrays):
        return [columns_grad(i % ny, F32 if i == ny else LOW, sides, *arrays) for i in range(2, ny + 1)]

    both_ffn = summed_core(part_ffn)
    far_sent = columns_grad(1, LOW, (1,), plane_ffn, [grad_gu])
    mix_parts = to_parts(after(normed_parts, plane_ffn))
    both_ffn, far_sent, plane_ffn, grad_gu, hidden, mix_parts, plane_cotangent, part_out = fence(
        both_ffn, far_sent, plane_ffn, grad_gu, hidden, mix_parts, plane_cotangent, part_out
    )

    grad_normed_ffn = summed_plane(both_ffn)
    near_sent = columns_grad(1, LOW, (0,), plane_ffn, [grad_gu])
    grad_gu_far = scatter_y(far_sent, columns_kept((1,), plane_ffn, [grad_gu]))
    (grad_down,) = call(
        rows_grad_kernel, [shape((units, width), LOW)], hidden, plane_cotangent, flops=2 * total * units * width,
    )
    both_out = summed_core(after(part_out, grad_down))
    grad_gu_far, grad_normed_ffn, near_sent, grad_down, plane_ffn, grad_gu, both_out = fence(
        grad_gu_far, grad_normed_ffn, near_sent, grad_down, plane_ffn, grad_gu, both_out
    )

    grad_gu_near = scatter_y(near_sent, columns_kept((0,), plane_ffn, [grad_gu]))
    grad_residual, branch, grad_parts = call(
        partial(branch_back_kernel, plan, part),
        [shape((rows, width)), shape((rows, width), LOW), shape(parts_shape, LOW)],
        where, grad_normed_ffn, cotangent, residual, mixed, full_gain_state, full_gain_ffn, w_out_full,
        specs=[SMEM] + [VMEM] * 7,
        scratch=[pltpu.VMEM((rows, width), LOW)],
        flops=2 * rows * width * width,
    )
    grads = to_parts(grad_parts)
    grad_gu_far = scatter_h(after(grad_gu_far, grads))
    output = (residual + summed_plane(after(both_out, grads))).astype(LOW)
    grads = by_group(to_cores(grads))
    mix_parts = to_cores(after(mix_parts, grads))
    (state_grad,) = call(
        mix_state_grad_kernel, [shape(states)], query_reach, grads,
        grid=(nx, heads), specs=[rows_spec, piece(0)], out_specs=[state_spec], flops=mix_flops // 4,
    )
    grad_gu_near, state_grad, grads, branch, grad_gu_far, output, grad_down, mix_parts = fence(
        grad_gu_near, state_grad, grads, branch, grad_gu_far, output, grad_down, mix_parts
    )

    next_grad = carry(state_grad, -1)
    grad_gu_near = scatter_h(after(grad_gu_near, next_grad))
    branch_pieces = from_plane([branch] * plane)
    df, dv, dq, lower_grad = call(
        mix_back_kernel,
        [shape(grouped, LOW)] * 3 + [shape((nx, heads, 8, HDIM))],
        where, *pre_args, lower, starts_wide, starts_row, cumulative, scores, grads, incoming, next_grad, decay,
        grid=(nx, heads),
        specs=[SMEM] + pre_specs + [head_spec, starts_spec, starts_row_spec, rows_spec, scores_spec]
        + [piece(0), state_spec, state_spec, state_spec],
        out_specs=[piece(0)] * 3 + [pl.BlockSpec((1, 1, 8, HDIM), lambda g, a: (g, a, 0, 0))],
        flops=12 * mix_flops,
    )
    pre_grads = [g.reshape(total, part) for g in (df, dv, dq)]
    three_sent = columns_grad(1, LOW, (0, 1), normed_in, pre_grads)
    (part_in,) = call(
        inputs_grad_kernel, [shape((total, width), LOW)], *after(pre_grads, three_sent), w_three, flops=project_flops
    )
    both_in = summed_core(part_in)
    three_kept = columns_kept((0, 1), normed_in, after(pre_grads, both_in))
    grad_three = scatter_y(three_sent, three_kept)
    both_in, grad_three, branch_pieces, grad_gu_near, grad_gu_far, grad_down = fence(
        both_in, grad_three, branch_pieces, grad_gu_near, grad_gu_far, grad_down
    )

    grad_normed_in = summed_plane(both_in)
    grad_three = scatter_h(grad_three)
    grad_down = scatter_y(*rows_of_y(grad_down.reshape(ny, nh, ffr, width)))
    (grad_out,) = call(
        rows_grad_kernel, [shape((part, width), LOW)], mix_parts.reshape(total, part), over_plane(branch_pieces),
        flops=2 * total * part * width,
    )
    grad_three, grad_normed_in, grad_gu_near, grad_out, grad_gu_far, grad_down = fence(
        grad_three, grad_normed_in, grad_gu_near, grad_out, grad_gu_far, grad_down
    )

    own_tokens = tokens.astype(F32)
    grad_tokens = grad_residual + norm_back(own_tokens, inverse_rms(own_tokens), grad_normed_in * full_gain_mix)
    grad_three = grad_three.astype(LOW).reshape(nx, nl, nc, r, 3 * part)
    grad_output = scatter_y(*rows_of_y(grad_out.reshape(ny, nh, r, width)))
    gu_blocks = collect([z.astype(LOW).reshape(nl, nc, r, 2 * units) for z in (grad_gu_near, grad_gu_far)])
    three_blocks = collect([after(grad_three[t], gu_blocks) for t in range(nx)])
    grad_down = scatter_h(grad_down)
    lower_grad = jnp.sum(lower_grad[:, :, 0], axis=0).reshape(1, part)
    lower_grad = sum(turns(after(lower_grad, grad_output), "y", ny))
    three_blocks, grad_output, gu_blocks, lower_grad = fence(
        three_blocks, grad_output, gu_blocks, lower_grad
    )

    grad_output = scatter_h(grad_output)
    lower_grad = sum(turns(after(lower_grad, grad_output), "h", nh))
    owners = []
    for j in range(ny):
        for p in range(nx):
            for i in range(nh):
                for o in range(nl):
                    for e in range(nc):
                        owners.append(((p * nl + o) * nc + e) * copies + j * nh + i)
    pairs = list(enumerate(owners))
    along = shape((r, HDIM))
    grad_w_gate, grad_w_up, along_ffn = call(
        partial(unpack_kernel, plan, ffr), [shape(w_gate.shape), shape(w_up.shape), along],
        where, to_cores(gu_blocks), w_gate, w_up, specs=[SMEM] + [VMEM] * 3,
        scratch=[pltpu.VMEM((nc, plane, r, 2 * units), LOW)],
    )
    grad_w_forget, grad_w_input, grad_w_query, along_mix = call(
        partial(unpack_part_kernel, plan, part), [shape(w_query.shape)] * 3 + [along],
        where, to_cores(three_blocks), w_forget, w_input, w_query, specs=[SMEM] + [VMEM] * 4,
    )
    grad_output = lax.ppermute(grad_output.astype(LOW), AXES, pairs).astype(F32)
    lower_grad = lax.dynamic_index_in_dim(lower_grad.reshape(copies, r), y * nh + h, 0, keepdims=False)
    lower_grad = lax.ppermute(lower_grad, AXES, pairs)
    grad_gain_mix = along_mix[:, 0] / gain_mix
    grad_gain_ffn = along_ffn[:, 0] / gain_ffn
    grad_gain_state = jnp.sum(w_output.astype(F32) * grad_output, axis=1) / gain_state
    return (
        output, grad_tokens, grad_w_query, grad_w_forget, grad_w_input, grad_output, grad_gain_mix, lower_grad,
        grad_gain_state, grad_w_gate, grad_w_up, grad_down, grad_gain_ffn,
    )


def solution(mesh):
    nb, ns, nc = (mesh.shape[a] for a in ("batch", "seq", "chip"))
    sizes = (nb // 2, 2, ns // 2, 2, nc)
    fine = jax.sharding.Mesh(mesh.devices.reshape(sizes), AXES)
    flat, matrix = P(AXES), P(AXES, None)
    return jax.shard_map(
        partial(body, Plan(sizes)),
        mesh=fine,
        in_specs=(
            matrix, flat, matrix, matrix, matrix, matrix, flat, flat, flat, matrix, matrix, matrix, flat, matrix,
        ),
        out_specs=(
            matrix, matrix, matrix, matrix, matrix, matrix, flat, flat, flat, matrix, matrix, matrix, flat,
        ),
        check_vma=False,
    )
```

```python
import math
from functools import partial

import jax
import jax.numpy as jnp
from jax import lax
from jax.experimental import pallas as pl
from jax.experimental.pallas import tpu as pltpu
from jax.sharding import PartitionSpec as P

HDIM = 128
EPSILON = 1e-06
RESET_LOG = -30.0
F32 = jnp.float32
LOW = jnp.bfloat16
AXES = ("y", "x", "h", "l", "chip")
LIMIT = 56 * 2**20
VMEM = pl.BlockSpec(memory_space=pltpu.VMEM)
SMEM = pl.BlockSpec(memory_space=pltpu.SMEM)
ANY = pl.BlockSpec(memory_space=pl.ANY)


def dot(left, right):
    return jnp.dot(left, right, preferred_element_type=F32)


def dot_tn(left, right):
    return lax.dot_general(left, right, (((0,), (0,)), ((), ())), preferred_element_type=F32)


def dot_nt(left, right):
    return lax.dot_general(left, right, (((1,), (1,)), ((), ())), preferred_element_type=F32)


def inverse_rms(values):
    return lax.rsqrt(jnp.mean(values * values, axis=-1, keepdims=True) + EPSILON)


def norm_back(values, rms, scaled):
    inner = jnp.mean(scaled * values, axis=-1, keepdims=True)
    return rms * scaled - values * (rms * rms * rms * inner)


def sigmoid(a):
    return 1.0 / (1.0 + jnp.exp(-a))


def pick(flag, first, second):
    return jnp.where(flag, first, second)


def after(x, *deps):
    return lax.optimization_barrier((x, deps))[0]


def shape(dims, dtype=F32):
    return jax.ShapeDtypeStruct(tuple(dims), dtype)


def call(kernel, outs, *args, specs=None, out_specs=None, grid=(), scratch=(), flops=0):
    outs = tuple(outs)
    specs = [VMEM] * len(args) if specs is None else specs
    out_specs = tuple([VMEM] * len(outs)) if out_specs is None else tuple(out_specs)
    moved = sum(math.prod(a.shape) * a.dtype.itemsize for a in (*args, *outs))
    return pl.pallas_call(
        kernel,
        out_shape=outs,
        grid=grid,
        in_specs=specs,
        out_specs=out_specs,
        scratch_shapes=list(scratch),
        compiler_params=pltpu.CompilerParams(vmem_limit_bytes=LIMIT),
        cost_estimate=pl.CostEstimate(flops=int(flops) // 8, bytes_accessed=int(moved) // 8, transcendentals=0),
    )(*args)


class Plan:
    def __init__(self, sizes):
        self.ny, self.nx, self.nh, self.nl, self.nc = sizes
        self.plane = self.nx * self.nl
        self.copies = self.ny * self.nh
        self.devices = self.copies * self.plane * self.nc

    def owner(self, y, p, h, c):
        return (((y * self.nx + p // self.nl) * self.nh + h) * self.nl + p % self.nl) * self.nc + c


def fetch(plan, where, blocks, target, sems, start=True):
    y, h, here = (where[i] for i in range(3))
    moves = []
    for t, (source, i, j, k, e) in enumerate(blocks):
        yy = lax.rem(y + (plan.ny - j), plan.ny)
        hh = lax.rem(h + (plan.nh - i), plan.nh)
        place = plan.owner(yy, here ^ k, hh, e)
        move = pltpu.make_async_copy(source, target.at[place], sems.at[t])
        if start:
            move.start()
        moves.append(move)
    return moves


def pack_kernel(plan, ffr, gate, up, out):
    units = plan.copies * ffr
    for e in range(plan.nc):
        for p in range(plan.plane):
            for w, base in ((gate, 0), (up, units)):
                for m in range(plan.copies):
                    at = plan.owner(m // plan.nh, p, m % plan.nh, e) * ffr
                    to = base + m * ffr
                    out[e, p, :, to : to + ffr] = w[:, at : at + ffr]


def unpack_kernel(plan, ffr, where, blocks, gate, up, grad_gate, grad_up, along, ordered):
    here = where[2]
    units = plan.copies * ffr
    for k in range(plan.plane):
        for e in range(plan.nc):
            ordered[e, here ^ k] = blocks[e, k]
    for e in range(plan.nc):
        for p in range(plan.plane):
            block = ordered[e, p].astype(F32)
            for g, base in ((grad_gate, 0), (grad_up, units)):
                for m in range(plan.copies):
                    at = plan.owner(m // plan.nh, p, m % plan.nh, e) * ffr
                    to = base + m * ffr
                    g[:, at : at + ffr] = block[:, to : to + ffr]
    total = jnp.sum(gate[...].astype(F32) * grad_gate[...], axis=1, keepdims=True)
    total = total + jnp.sum(up[...].astype(F32) * grad_up[...], axis=1, keepdims=True)
    along[...] = jnp.broadcast_to(total, along.shape)


def unpack_part_kernel(plan, part, where, blocks, w0, w1, w2, g0, g1, g2, along):
    here = where[2]
    for k in range(plan.plane):
        for e in range(plan.nc):
            at = pl.multiple_of(((here ^ k) * plan.nc + e) * part, part)
            for i, g in enumerate((g0, g1, g2)):
                g[:, pl.ds(at, part)] = blocks[e, k, :, i * part : (i + 1) * part].astype(F32)
    total = 0.0
    for w, g in ((w0, g0), (w1, g1), (w2, g2)):
        total = total + jnp.sum(w[...].astype(F32) * g[...], axis=1, keepdims=True)
    along[...] = jnp.broadcast_to(total, along.shape)


def normalize(x, gain, out, step):
    @pl.loop(0, x.shape[0] // step)
    def _(t):
        at = pl.ds(pl.multiple_of(t * step, step), step)
        values = x[at, :].astype(F32)
        out[at, :] = (values * inverse_rms(values) * gain[...]).astype(LOW)


def project_kernel(plan, names, where, x, gain, *rest):
    blocks, (normed, pre, weight, sems) = rest[: len(names)], rest[len(names) :]
    moves = fetch(
        plan, where,
        [(ref.at[k * plan.nc + e], i, j, k, e) for ref, (i, j) in zip(blocks, names)
         for k in range(plan.plane) for e in range(plan.nc)],
        weight, sems,
    )
    normalize(x, gain, normed, 64)
    for move in moves:
        move.wait()
    pre[...] = dot(normed[...], weight[...].reshape(-1, weight.shape[-1]))


def ffn_kernel(plan, names, where, normed, cotangent, down, *rest):
    blocks, (hidden, grad_gu, part_out, part_grad, weight, sems) = rest[: len(names)], rest[len(names) :]
    first = pl.program_id(0) == 0

    def moves(start):
        return fetch(
            plan, where,
            [(ref.at[i, k * plan.nc + e], i, j, base + k, e) for ref, (j, base) in zip(blocks, names)
             for i in range(plan.nh) for k in range(ref.shape[1] // plan.nc) for e in range(plan.nc)],
            weight, sems, start,
        )

    @pl.when(first)
    def _():
        moves(True)

    units = down.shape[0]
    upstream = dot_nt(cotangent[...], down[...])

    @pl.when(first)
    def _():
        for move in moves(False):
            move.wait()

    full = weight[...].reshape(-1, weight.shape[-1])
    both = dot(normed[...], full)
    gate, up = both[:, :units], both[:, units:]
    sig = sigmoid(gate)
    silu = gate * sig
    hid = (silu * up).astype(LOW)
    hidden[...] = hid
    grad_gu[:, :units] = (upstream * up * sig * (1.0 + gate * (1.0 - sig))).astype(LOW)
    grad_gu[:, units:] = (upstream * silu).astype(LOW)
    part_grad[...] = dot_nt(grad_gu[...], full).astype(part_grad.dtype)
    part_out[...] = dot(hid, down[...]).astype(part_out.dtype)


def columns_grad_kernel(plan, turn, sides, count, where, normed, *rest):
    grads, out = rest[:count], rest[count]
    y = lax.rem(where[0] + (plan.ny - turn), plan.ny)
    step = out.shape[0] * out.shape[2]
    for t, side in enumerate(sides):
        at = pl.multiple_of((y * plan.nx + (where[5] ^ side)) * step, step)
        base = 0
        for a in grads:
            n = a.shape[1]
            value = dot_tn(normed[:, pl.ds(at, step)], a[...])
            for i in range(plan.nh):
                out[i, t, :, base : base + n] = value[i * out.shape[2] : (i + 1) * out.shape[2]].astype(out.dtype)
            base += n


def rows_grad_kernel(left, right, out):
    n = 512
    for t in range(out.shape[1] // n):
        at = slice(t * n, (t + 1) * n)
        out[:, at] = dot_tn(left[...], right[:, at]).astype(out.dtype)


def interleaved(x):
    return jnp.concatenate([x[e, 0, i] for i in range(x.shape[2]) for e in range(x.shape[0])], axis=0)


def separated(x, out):
    nc, _, nl, rows, _ = out.shape
    for i in range(nl):
        for e in range(nc):
            at = (i * nc + e) * rows
            out[e, 0, i] = x[at : at + rows].astype(out.dtype)


def thirds(x):
    first = x.astype(LOW)
    rest = x - first.astype(F32)
    second = rest.astype(LOW)
    return first, second, (rest - second.astype(F32)).astype(LOW)


def causal_of(where, span, rows):
    flip = where[4] * rows
    t = lax.broadcasted_iota(jnp.int32, (span, span), 0) ^ flip
    s = lax.broadcasted_iota(jnp.int32, (span, span), 1) ^ flip
    return (t >= s).astype(F32)


def gate_terms(forget_pre, lower, is_start):
    sig = sigmoid(forget_pre)
    gate = lower + (1.0 - lower) * sig
    return sig, gate, 1.0 - gate, jnp.where(is_start, 0.0, jnp.log(gate))


def decay_terms(causal, starts, starts_row, cumulative, total):
    low = causal.astype(LOW)
    count = dot(low, starts)
    count_row = dot_nt(starts_row, low)[:1]
    ends = jnp.sum(starts.astype(F32), axis=0, keepdims=True)
    reach = jnp.exp(RESET_LOG * count)
    left = jnp.exp(RESET_LOG * (ends - count))
    between = causal * jnp.exp(RESET_LOG * jnp.maximum(count[:, :1] - count_row, 0.0))
    return reach, between, jnp.exp(cumulative), jnp.exp(-cumulative), jnp.exp(total - cumulative) * left, ends


def mix_kernel(
    where, f, v, q, lower, starts, starts_row,
    end_state, decay, local, query_reach, cumulative_out, scores_out,
):
    rows = f.shape[3]
    forget_pre, value, query_pre = interleaved(f), interleaved(v), interleaved(q)
    span = forget_pre.shape[0]
    is_start = starts[0].astype(F32) == 1.0
    _, _, key, log_decay = gate_terms(forget_pre, lower[0], is_start)
    causal = causal_of(where, span, rows)
    low = causal.astype(LOW)
    parts = thirds(log_decay)
    cumulative = dot(low, parts[0]) + dot(low, parts[1]) + dot(low, parts[2])
    total = jnp.sum(log_decay, axis=0, keepdims=True)
    reach, between, grow, shrink, suffix, ends = decay_terms(causal, starts[0], starts_row[0], cumulative, total)
    query = query_pre * sigmoid(query_pre) * grow
    value_low = value.astype(LOW)
    end_state[0, 0] = dot_tn((key * suffix).astype(LOW), value_low)
    ones = jnp.ones((span, HDIM), LOW)
    total_column = dot_tn(parts[0], ones) + dot_tn(parts[1], ones) + dot_tn(parts[2], ones)
    decay[0, 0] = jnp.exp(total_column + RESET_LOG * ends)
    scores = (dot_nt(query.astype(LOW), (key * shrink).astype(LOW)) * between).astype(LOW)
    local[0, 0] = dot(scores, value_low)
    query_reach[0, 0] = (query * reach).astype(LOW)
    cumulative_out[0, 0] = cumulative
    scores_out[0, 0] = scores


def mix_end_kernel(local, query_reach, incoming, out):
    separated(local[0, 0] + dot(query_reach[0, 0], incoming[0, 0]), out)


def mix_state_grad_kernel(query_reach, grads, out):
    out[0, 0] = dot_tn(query_reach[0, 0], interleaved(grads))


def mix_back_kernel(
    where, f, v, q, lower, starts, starts_row, cumulative_in, scores_in, grads, incoming, next_grad, decay,
    df, dv, dq, lower_grad,
):
    rows = f.shape[3]
    forget_pre, value, query_pre, upstream = interleaved(f), interleaved(v), interleaved(q), interleaved(grads)
    span = forget_pre.shape[0]
    is_start = starts[0].astype(F32) == 1.0
    low_bound = lower[0]
    forget_sig, gate, key, log_decay = gate_terms(forget_pre, low_bound, is_start)
    causal = causal_of(where, span, rows)
    low = causal.astype(LOW)
    cumulative = cumulative_in[0, 0]
    total = jnp.sum(log_decay, axis=0, keepdims=True)
    reach, between, grow, shrink, suffix, _ = decay_terms(causal, starts[0], starts_row[0], cumulative, total)
    query_sig = sigmoid(query_pre)
    query_ext = (query_pre * query_sig * grow).astype(LOW)
    key_shrink = (key * shrink).astype(LOW)
    key_suffix = (key * suffix).astype(LOW)
    value_low = value.astype(LOW)
    state, after_state = incoming[0, 0], next_grad[0, 0]
    grad_scores = (dot_nt(upstream, value_low) * between).astype(LOW)
    grad_ext = dot(grad_scores, key_shrink) + reach * dot_nt(upstream, state)
    grad_shrink = dot_tn(grad_scores, query_ext)
    grad_suffix = dot_nt(value_low, after_state)
    grad_value = dot_tn(scores_in[0, 0], upstream) + dot(key_suffix, after_state)
    suffix_term = key_suffix.astype(F32) * grad_suffix
    terms = query_ext.astype(F32) * grad_ext - key_shrink.astype(F32) * grad_shrink - suffix_term
    ones = jnp.ones((8, HDIM), LOW)
    state_term = thirds(decay[0, 0] * state.astype(F32) * after_state.astype(F32))
    state_row = (dot_nt(ones, state_term[0]) + dot_nt(ones, state_term[1]) + dot_nt(ones, state_term[2]))[:1]
    grad_total = jnp.sum(suffix_term, axis=0, keepdims=True) + state_row
    parts = thirds(terms)
    grad_log = dot_tn(low, parts[0]) + dot_tn(low, parts[1]) + dot_tn(low, parts[2]) + grad_total
    grad_key = grad_shrink * shrink + grad_suffix * suffix
    grad_forget = jnp.where(is_start, 0.0, grad_log / gate) - grad_key
    lower_grad[0, 0] = jnp.broadcast_to(
        jnp.sum(grad_forget * (1.0 - forget_sig), axis=0, keepdims=True), lower_grad.shape[2:]
    )
    separated(grad_forget * (1.0 - low_bound) * forget_sig * (1.0 - forget_sig), df)
    separated(grad_value, dv)
    separated(grad_ext * grow * query_sig * (1.0 + query_pre * (1.0 - query_sig)), dq)


def branch_kernel(plan, names, part, where, tokens, gain_state, gain_ffn, *rest):
    mixed_in, rest = rest[: plan.plane], rest[plan.plane :]
    own, other, mixed, normed_parts, residual, normed_ffn, weight, sems = rest
    here = where[2]
    moves = fetch(
        plan, where,
        [(ref.at[t, u, m], i, j, k, e) for ref, e in ((own, where[3]), (other, where[3] ^ 1)) for t, u, m, i, j, k in names],
        weight, sems,
    )
    for k in range(plan.plane):
        for e in range(plan.nc):
            at = pl.multiple_of(((here ^ k) * plan.nc + e) * part, part)
            mixed[:, pl.ds(at, part)] = mixed_in[k][e].astype(F32)
    values = mixed[...]
    normed = (values * inverse_rms(values) * gain_state[...]).astype(LOW)
    normed_ffn[...] = normed
    for k in range(plan.plane):
        for e in range(plan.nc):
            at = pl.multiple_of(((here ^ k) * plan.nc + e) * part, part)
            normed_parts[k, e] = normed_ffn[:, pl.ds(at, part)]
    for move in moves:
        move.wait()
    total = tokens[...].astype(F32) + dot(normed, weight[...].reshape(-1, weight.shape[-1]))
    residual[...] = total
    normed_ffn[...] = (total * inverse_rms(total) * gain_ffn[...]).astype(LOW)


def branch_back_kernel(
    plan, part, where, upstream, cotangent, residual, mixed, gain_state, gain_ffn, weight,
    grad_residual, branch, grad_parts, scratch,
):
    here = where[2]
    values = residual[...]
    grad = cotangent[...].astype(F32) + norm_back(values, inverse_rms(values), upstream[...] * gain_ffn[...])
    grad_residual[...] = grad
    low = grad.astype(LOW)
    branch[...] = low
    values = mixed[...]
    scaled = dot_nt(low, weight[...].reshape(-1, weight.shape[-1])) * gain_state[...]
    scratch[...] = norm_back(values, inverse_rms(values), scaled).astype(LOW)
    for k in range(plan.plane):
        for e in range(plan.nc):
            at = pl.multiple_of(((here ^ k) * plan.nc + e) * part, part)
            grad_parts[k, e] = scratch[:, pl.ds(at, part)]


def inputs_grad_kernel(df, dv, dq, weight, out):
    part = df.shape[1]
    full = weight[...].reshape(-1, weight.shape[-1])
    out[...] = (
        dot_nt(df[...], full[:, :part]) + dot_nt(dv[...], full[:, part : 2 * part])
        + dot_nt(dq[...], full[:, 2 * part :])
    ).astype(out.dtype)


def body(
    plan, tokens, starts, w_query, w_forget, w_input, w_output, gain_mix, lower_bound, gain_state,
    w_gate, w_up, w_down, gain_ffn, cotangent,
):
    ny, nx, nh, nl, nc, plane, copies = (
        plan.ny, plan.nx, plan.nh, plan.nl, plan.nc, plan.plane, plan.copies
    )
    y, x_, h, l, c = (lax.axis_index(a) for a in AXES)
    here = x_ * nl + l
    where = jnp.stack([y, h, here, c, l * nc, x_]).astype(jnp.int32)
    rows, width = tokens.shape
    r = w_query.shape[0]
    part = width // (plane * nc)
    ffr = w_down.shape[0]
    units = copies * ffr
    heads = part // HDIM
    span = nl * nc * rows
    half = plane * rows
    names = [(i, j) for i in range(nh) for j in range(ny)]

    def fence(*values):
        return lax.optimization_barrier(values)

    def from_plane(blocks):
        return [blocks[0]] + [
            lax.ppermute(blocks[k], ("x", "l"), [(i, i ^ k) for i in range(plane)]) for k in range(1, plane)
        ]

    def swap(x, axis):
        return lax.ppermute(x, axis, [(0, 1), (1, 0)])

    def to_cores(x):
        return lax.all_to_all(x, "chip", 0, 0, tiled=True)

    def turn(x, axis, n):
        return lax.ppermute(x, axis, [(i, (i + 1) % n) for i in range(n)])

    def turns(x, axis, n):
        out = [x]
        for _ in range(1, n):
            out.append(turn(out[-1], axis, n))
        return out

    def over_plane(pieces):
        mine = jnp.concatenate(pieces)
        return to_cores(jnp.stack([mine, mine])).reshape(nc * mine.shape[0], -1)

    def summed_core(x):
        x = to_cores(x.reshape(nc, plane, rows, -1))
        sums = [x[0, k].astype(F32) + x[1, k].astype(F32) for k in range(plane)]
        return [sums[0]] + [z.astype(LOW) for z in sums[1:]]

    def summed_plane(sums):
        got = from_plane(sums)
        return sum((z.astype(F32) for z in got[1:]), got[0])

    def at_plane(x, axis):
        return [lax.dynamic_index_in_dim(x, here ^ k, axis, keepdims=False) for k in range(plane)]

    def collect(sides):
        got = from_plane(
            [lax.dynamic_index_in_dim(sides[k // nl], l ^ (k % nl), 0, keepdims=False) for k in range(plane)]
        )
        return jnp.stack(got, axis=1)

    def to_parts(x):
        return jnp.stack(from_plane([x[k] for k in range(plane)]), axis=1)

    def scatter_y(sent, kept):
        total = sent
        for i, mine in enumerate(kept):
            total = turn(total, "y", ny).astype(F32) + mine.astype(F32)
            total = total.astype(LOW) if i < len(kept) - 1 else total
        return total

    def scatter_h(x):
        def block(i):
            return lax.dynamic_index_in_dim(x, (h - i) % nh, 0, keepdims=False)

        total = block(1 % nh)
        for i in range(2, nh + 1):
            total = turn(total.astype(LOW), "h", nh).astype(F32) + block(i % nh)
        return total

    def rows_of_y(x):
        out = [lax.dynamic_index_in_dim(x, (y - i) % ny, 0, keepdims=False) for i in range(1, ny + 1)]
        return out[0], out[1:]

    spread = lambda w: w.reshape(r, plane, nc, part)
    three = jnp.concatenate([spread(w_forget), spread(w_input), spread(w_query)], axis=3).transpose(2, 1, 0, 3)
    three = to_cores(three)
    three = jnp.concatenate(from_plane(at_plane(three, 1)))
    small = jnp.concatenate([gain_mix, gain_state, gain_ffn, lower_bound, starts.astype(F32)]).reshape(1, -1)
    small_mine = jnp.concatenate(from_plane([after(small, three)] * plane))
    small_other = lax.ppermute(small_mine, "chip", [(i, i ^ 1) for i in range(nc)])
    plane_small = jnp.concatenate([pick(c == 0, small_mine, small_other), pick(c == 0, small_other, small_mine)])
    out_first = turns(w_output, "y", ny)
    tokens_pair = jnp.concatenate([tokens, swap(tokens, "l")])
    vectors = jnp.stack(turns(plane_small[:, : 4 * r], "y", ny))
    vectors = jnp.concatenate(turns(vectors, "h", nh)).reshape(plan.devices, -1)
    (packed,) = call(partial(pack_kernel, plan, ffr), [shape((nc, plane, r, 2 * units), LOW)], w_gate, w_up)
    packed = to_cores(packed)
    plane_small, three, w_output, out_first, tokens_pair, packed, vectors, cotangent, w_down = fence(
        plane_small, three, w_output, out_first, tokens_pair, packed, vectors, cotangent, w_down
    )

    three_line = turns(three, "h", nh)
    three_first = turns(three, "y", ny)
    out_line = turns(after(w_output, three_line), "h", nh)
    tokens_far = swap(tokens_pair, "x")
    gate_up = from_plane(at_plane(packed, 1))
    gate_up = [jnp.concatenate(gate_up[:nl]), jnp.concatenate(gate_up[nl:])]
    three_line, three_first, out_line, tokens_pair, tokens_far, gate_up, cotangent, w_down = fence(
        three_line, three_first, out_line, tokens_pair, tokens_far, gate_up, cotangent, w_down
    )

    three = three_first + [z for x in three_line[1:] for z in turns(x, "y", ny)]
    out_copies = out_first + [z for x in out_line[1:] for z in turns(x, "y", ny)]
    gu_line = turns(gate_up[0], "h", nh)
    plane_tokens = over_plane([tokens_pair, tokens_far])
    plane_starts = (
        plane_small[:, 4 * r :].reshape(nc, nx, nl, rows).transpose(1, 2, 0, 3).reshape(nx, span)
    )
    starts_row = jnp.broadcast_to(plane_starts[:, None], (nx, 8, span)).astype(LOW)
    starts_wide = jnp.broadcast_to(plane_starts[:, :, None], (nx, span, HDIM)).astype(LOW)
    places = jnp.stack([
        plan.owner((y - j) % ny, here ^ k, (h - i) % nh, e)
        for i in range(nh) for j in range(ny) for e in range(nc) for k in range(plane)
    ])
    ordered = (jnp.arange(plan.devices)[:, None] == places[None, :]).astype(F32)
    vectors = jnp.dot(ordered, vectors, precision=lax.Precision.HIGHEST)
    vectors = vectors.reshape(plan.devices, 4, r).transpose(1, 0, 2).reshape(4, width)
    full_gain_mix, full_gain_state, full_gain_ffn = (vectors[i : i + 1] for i in range(3))
    lower = lax.dynamic_slice_in_dim(vectors[3], (here * nc + c) * part, part).reshape(heads, 1, HDIM)
    count = plan.devices
    total = nc * half
    project_flops = 2 * total * width * 3 * part
    normed_in, pre, w_three = call(
        partial(project_kernel, plan, names),
        [shape((total, width), LOW), shape((total, 3 * part)), shape((count, r, 3 * part), LOW)],
        where, plane_tokens, full_gain_mix, *three,
        specs=[SMEM, VMEM, VMEM] + [ANY] * copies,
        scratch=[pltpu.SemaphoreType.DMA((count,))],
        flops=project_flops,
    )
    gu_first = jnp.stack(after(gu_line, pre))
    cut = copies // 2
    pieces = [jnp.stack(out_copies[:cut]), jnp.stack(out_copies[cut:])]
    moved = [swap(z, axis) for z, axis in zip(pieces, ("l", "x"))]
    cotangent_pair = jnp.concatenate([cotangent, swap(after(cotangent, moved), "l")])
    gate_up, pre, pieces, moved, lower, starts_wide, starts_row, gu_first, cotangent_pair, w_down = fence(
        gate_up, pre, pieces, moved, lower, starts_wide, starts_row, gu_first, cotangent_pair, w_down
    )

    by_group = lambda x: x.reshape(nc, nx, nl, rows, -1)
    piece = lambda i: pl.BlockSpec((nc, 1, nl, rows, HDIM), lambda g, a, i=i: (0, g, 0, 0, i * heads + a))
    state_spec = pl.BlockSpec((1, 1, HDIM, HDIM), lambda g, a: (g, a, 0, 0))
    rows_spec = pl.BlockSpec((1, 1, span, HDIM), lambda g, a: (g, a, 0, 0))
    scores_spec = pl.BlockSpec((1, 1, span, span), lambda g, a: (g, a, 0, 0))
    head_spec = pl.BlockSpec((1, 1, HDIM), lambda g, a: (a, 0, 0))
    starts_spec = pl.BlockSpec((1, span, HDIM), lambda g, a: (g, 0, 0))
    starts_row_spec = pl.BlockSpec((1, 8, span), lambda g, a: (g, 0, 0))
    pre_args = (by_group(pre),) * 3
    pre_specs = [piece(0), piece(1), piece(2)]
    states = (nx, heads, HDIM, HDIM)
    by_row = (nx, heads, span, HDIM)
    grouped = (nc, nx, nl, rows, part)
    mix_flops = nx * heads * 2 * span * span * HDIM
    end_state, decay, local, query_reach, cumulative, scores = call(
        mix_kernel,
        [shape(states), shape(states), shape(by_row), shape(by_row, LOW), shape(by_row),
         shape((nx, heads, span, span), LOW)],
        where, *pre_args, lower, starts_wide, starts_row,
        grid=(nx, heads),
        specs=[SMEM] + pre_specs + [head_spec, starts_spec, starts_row_spec],
        out_specs=[state_spec, state_spec, rows_spec, rows_spec, rows_spec, scores_spec],
        flops=8 * mix_flops,
    )
    gu_first = turns(gu_first, "y", ny)
    gu_second = turns(gate_up[1], "h", nh)
    pairs = [jnp.stack([a, z]) for a, z in zip(pieces, moved)]
    moved = [swap(z, axis) for z, axis in zip(pairs, ("x", "l"))]
    groups = [pairs[0], moved[0], pairs[1], moved[1]]
    out_names = [
        (t * 2 + distance, u, m, *names[t * cut + m], u * nl + distance if t else distance * nl + u)
        for t in range(2) for distance in range(2) for u in range(2) for m in range(cut)
    ]
    end_state, decay, local, query_reach, gu_first, groups, gu_second, cotangent_pair, w_down = fence(
        end_state, decay, local, query_reach, gu_first, groups, gu_second, cotangent_pair, w_down
    )

    def carry(block, step):
        incoming = jnp.zeros_like(block)
        for t in range(nh - 1):
            pairs = [(i, i + step) for i in range(nh) if 0 <= i + step < nh]
            sent = decay * incoming + block if t else block
            incoming = lax.ppermute(sent.astype(LOW), "h", pairs)
            incoming = incoming if t == nh - 2 else incoming.astype(F32)
        return incoming

    incoming = carry(end_state, 1)
    groups, gu_second = (jnp.stack(z) for z in after((groups, gu_second), incoming))
    (mixed,) = call(
        mix_end_kernel, [shape(grouped, LOW)], local, query_reach, incoming,
        grid=(nx, heads), specs=[rows_spec, rows_spec, state_spec], out_specs=[piece(0)], flops=mix_flops // 4,
    )
    mixed = to_cores(mixed.reshape(nc, plane, rows, part))
    down_line = turns(after(w_down, incoming), "h", nh)
    mixed_in = from_plane(after([mixed[:, k] for k in range(plane)], down_line))
    gate_up = gu_first + turns(gu_second, "y", ny)
    cotangent_far = swap(cotangent_pair, "x")
    groups_other = lax.ppermute(groups, "chip", [(i, i ^ 1) for i in range(nc)])
    plane_cotangent = over_plane([cotangent_pair, cotangent_far])
    mixed_in, gate_up, groups, groups_other, plane_cotangent, down_line = fence(
        mixed_in, gate_up, groups, groups_other, plane_cotangent, down_line
    )

    parts_shape = (plane, nc, rows, part)
    mixed, normed_parts, residual, normed_ffn, w_out_full = call(
        partial(branch_kernel, plan, out_names, part),
        [shape((rows, width)), shape(parts_shape, LOW), shape((rows, width)), shape((rows, width), LOW),
         shape((count, r, width), LOW)],
        where, tokens, full_gain_state, full_gain_ffn, *mixed_in, groups, groups_other,
        specs=[SMEM] + [VMEM] * (3 + plane) + [ANY] * 2,
        scratch=[pltpu.SemaphoreType.DMA((count,))],
        flops=2 * rows * width * width,
    )
    ffn_pieces = from_plane([normed_ffn] * plane)
    down = jnp.zeros((ny, nh, ffr, width), LOW)
    for j, blocks in enumerate(turns(jnp.stack(down_line), "y", ny)):
        for i in range(nh):
            down = lax.dynamic_update_slice(down, blocks[i][None, None], ((y - j) % ny, (h - i) % nh, 0, 0))
    down = down.reshape(units, width)
    ffn_pieces, gate_up, down, normed_parts, plane_cotangent = fence(
        ffn_pieces, gate_up, down, normed_parts, plane_cotangent
    )

    plane_ffn = over_plane(ffn_pieces)
    gu_names = [(j, k) for k in (0, nl) for j in range(ny)]
    step = half
    row_spec = lambda n: pl.BlockSpec((step, n), lambda t: (t, 0))
    hidden, grad_gu, part_out, part_ffn = call(
        partial(ffn_kernel, plan, gu_names),
        [shape((total, units), LOW), shape((total, 2 * units), LOW), shape((total, width), LOW),
         shape((total, width), LOW)],
        where, plane_ffn, plane_cotangent, down, *gate_up,
        grid=(total // step,),
        specs=[SMEM, row_spec(width), row_spec(width), VMEM] + [ANY] * len(gate_up),
        out_specs=[row_spec(units), row_spec(2 * units), row_spec(width), row_spec(width)],
        scratch=[pltpu.VMEM((count, r, 2 * units), LOW), pltpu.SemaphoreType.DMA((count,))],
        flops=2 * total * width * units * 7,
    )
    lcr = nl * nc * r

    def columns_grad(turns, dtype, sides, normed, grads):
        n = sum(g.shape[1] for g in grads)
        return call(
            partial(columns_grad_kernel, plan, turns, sides, len(grads)), [shape((nh, len(sides), lcr, n), dtype)],
            where, normed, *grads, specs=[SMEM] + [VMEM] * (1 + len(grads)),
            flops=2 * total * width * n * len(sides) // (ny * nx),
        )[0]

    def columns_kept(sides, *arrays):
        return [columns_grad(i % ny, F32 if i == ny else LOW, sides, *arrays) for i in range(2, ny + 1)]

    both_ffn = summed_core(part_ffn)
    far_sent = columns_grad(1, LOW, (1,), plane_ffn, [grad_gu])
    mix_parts = to_parts(after(normed_parts, plane_ffn))
    both_ffn, far_sent, plane_ffn, grad_gu, hidden, mix_parts, plane_cotangent, part_out = fence(
        both_ffn, far_sent, plane_ffn, grad_gu, hidden, mix_parts, plane_cotangent, part_out
    )

    grad_normed_ffn = summed_plane(both_ffn)
    near_sent = columns_grad(1, LOW, (0,), plane_ffn, [grad_gu])
    grad_gu_far = scatter_y(far_sent, columns_kept((1,), plane_ffn, [grad_gu]))
    (grad_down,) = call(
        rows_grad_kernel, [shape((units, width), LOW)], hidden, plane_cotangent, flops=2 * total * units * width,
    )
    both_out = summed_core(after(part_out, grad_down))
    grad_gu_far, grad_normed_ffn, near_sent, grad_down, plane_ffn, grad_gu, both_out = fence(
        grad_gu_far, grad_normed_ffn, near_sent, grad_down, plane_ffn, grad_gu, both_out
    )

    grad_gu_near = scatter_y(near_sent, columns_kept((0,), plane_ffn, [grad_gu]))
    grad_residual, branch, grad_parts = call(
        partial(branch_back_kernel, plan, part),
        [shape((rows, width)), shape((rows, width), LOW), shape(parts_shape, LOW)],
        where, grad_normed_ffn, cotangent, residual, mixed, full_gain_state, full_gain_ffn, w_out_full,
        specs=[SMEM] + [VMEM] * 7,
        scratch=[pltpu.VMEM((rows, width), LOW)],
        flops=2 * rows * width * width,
    )
    grads = to_parts(grad_parts)
    grad_gu_far = scatter_h(after(grad_gu_far, grads))
    output = (residual + summed_plane(after(both_out, grads))).astype(LOW)
    grads = by_group(to_cores(grads))
    mix_parts = to_cores(after(mix_parts, grads))
    (state_grad,) = call(
        mix_state_grad_kernel, [shape(states)], query_reach, grads,
        grid=(nx, heads), specs=[rows_spec, piece(0)], out_specs=[state_spec], flops=mix_flops // 4,
    )
    grad_gu_near, state_grad, grads, branch, grad_gu_far, output, grad_down, mix_parts = fence(
        grad_gu_near, state_grad, grads, branch, grad_gu_far, output, grad_down, mix_parts
    )

    next_grad = carry(state_grad, -1)
    grad_gu_near = scatter_h(after(grad_gu_near, next_grad))
    branch_pieces = from_plane([branch] * plane)
    df, dv, dq, lower_grad = call(
        mix_back_kernel,
        [shape(grouped, LOW)] * 3 + [shape((nx, heads, 8, HDIM))],
        where, *pre_args, lower, starts_wide, starts_row, cumulative, scores, grads, incoming, next_grad, decay,
        grid=(nx, heads),
        specs=[SMEM] + pre_specs + [head_spec, starts_spec, starts_row_spec, rows_spec, scores_spec]
        + [piece(0), state_spec, state_spec, state_spec],
        out_specs=[piece(0)] * 3 + [pl.BlockSpec((1, 1, 8, HDIM), lambda g, a: (g, a, 0, 0))],
        flops=12 * mix_flops,
    )
    pre_grads = [g.reshape(total, part) for g in (df, dv, dq)]
    three_sent = columns_grad(1, LOW, (0, 1), normed_in, pre_grads)
    (part_in,) = call(
        inputs_grad_kernel, [shape((total, width), LOW)], *after(pre_grads, (three_sent, branch_pieces)), w_three, flops=project_flops
    )
    both_in = summed_core(part_in)
    three_kept = columns_kept((0, 1), normed_in, after(pre_grads, both_in))
    grad_three = scatter_y(three_sent, three_kept)
    both_in, grad_three, branch_pieces, grad_gu_near, grad_gu_far, grad_down = fence(
        both_in, grad_three, branch_pieces, grad_gu_near, grad_gu_far, grad_down
    )

    grad_normed_in = summed_plane(both_in)
    grad_three = scatter_h(grad_three)
    grad_down = scatter_y(*rows_of_y(grad_down.reshape(ny, nh, ffr, width)))
    (grad_out,) = call(
        rows_grad_kernel, [shape((part, width), LOW)], mix_parts.reshape(total, part), over_plane(branch_pieces),
        flops=2 * total * part * width,
    )
    grad_three, grad_normed_in, grad_gu_near, grad_out, grad_gu_far, grad_down = fence(
        grad_three, grad_normed_in, grad_gu_near, grad_out, grad_gu_far, grad_down
    )

    own_tokens = tokens.astype(F32)
    grad_tokens = grad_residual + norm_back(own_tokens, inverse_rms(own_tokens), grad_normed_in * full_gain_mix)
    grad_three = grad_three.astype(LOW).reshape(nx, nl, nc, r, 3 * part)
    grad_output = scatter_y(*rows_of_y(grad_out.reshape(ny, nh, r, width)))
    gu_blocks = collect([z.astype(LOW).reshape(nl, nc, r, 2 * units) for z in (grad_gu_near, grad_gu_far)])
    three_blocks = collect([after(grad_three[t], gu_blocks) for t in range(nx)])
    along = shape((r, HDIM))
    grad_w_gate, grad_w_up, along_ffn = call(
        partial(unpack_kernel, plan, ffr), [shape(w_gate.shape), shape(w_up.shape), along],
        where, to_cores(gu_blocks), w_gate, w_up, specs=[SMEM] + [VMEM] * 3,
        scratch=[pltpu.VMEM((nc, plane, r, 2 * units), LOW)],
    )
    grad_down = scatter_h(grad_down)
    lower_grad = jnp.sum(lower_grad[:, :, 0], axis=0).reshape(1, part)
    lower_grad = sum(turns(after(lower_grad, grad_output), "y", ny))
    three_blocks, grad_output, lower_grad, grad_w_gate, grad_w_up, along_ffn = fence(
        three_blocks, grad_output, lower_grad, grad_w_gate, grad_w_up, along_ffn
    )

    grad_output = scatter_h(grad_output)
    lower_grad = sum(turns(after(lower_grad, grad_output), "h", nh))
    owners = []
    for j in range(ny):
        for p in range(nx):
            for i in range(nh):
                for o in range(nl):
                    for e in range(nc):
                        owners.append(((p * nl + o) * nc + e) * copies + j * nh + i)
    pairs = list(enumerate(owners))
    grad_w_forget, grad_w_input, grad_w_query, along_mix = call(
        partial(unpack_part_kernel, plan, part), [shape(w_query.shape)] * 3 + [along],
        where, to_cores(three_blocks), w_forget, w_input, w_query, specs=[SMEM] + [VMEM] * 4,
    )
    grad_output = lax.ppermute(grad_output.astype(LOW), AXES, pairs).astype(F32)
    lower_grad = lax.dynamic_index_in_dim(lower_grad.reshape(copies, r), y * nh + h, 0, keepdims=False)
    lower_grad = lax.ppermute(lower_grad, AXES, pairs)
    grad_gain_mix = along_mix[:, 0] / gain_mix
    grad_gain_ffn = along_ffn[:, 0] / gain_ffn
    grad_gain_state = jnp.sum(w_output.astype(F32) * grad_output, axis=1) / gain_state
    return (
        output, grad_tokens, grad_w_query, grad_w_forget, grad_w_input, grad_output, grad_gain_mix, lower_grad,
        grad_gain_state, grad_w_gate, grad_w_up, grad_down, grad_gain_ffn,
    )


def solution(mesh):
    nb, ns, nc = (mesh.shape[a] for a in ("batch", "seq", "chip"))
    sizes = (nb // 2, 2, ns // 2, 2, nc)
    fine = jax.sharding.Mesh(mesh.devices.reshape(sizes), AXES)
    flat, matrix = P(AXES), P(AXES, None)
    return jax.shard_map(
        partial(body, Plan(sizes)),
        mesh=fine,
        in_specs=(
            matrix, flat, matrix, matrix, matrix, matrix, flat, flat, flat, matrix, matrix, matrix, flat, matrix,
        ),
        out_specs=(
            matrix, matrix, matrix, matrix, matrix, matrix, flat, flat, flat, matrix, matrix, matrix, flat,
        ),
        check_vma=False,
    )
```
